256 devices in a mesh: pb: 64 (over x_hi, y, z), ka: 4 (over x_lo, core).
Axes of the slice: x: 4 (x_hi: 2, x_lo: 2; x = x_hi * 2 + x_lo), y: 4, z: 8, core: 2. Of those that a mesh axis runs over, the one named last changes fastest.
Arguments:
- queries: bfloat16 [32768, 1024], P('pb'), may hold values from -9 to 9
- keys: bfloat16 [8, 4096, 128], P(None, 'ka'), may hold values from -6 to 6
- values: bfloat16 [8, 4096, 128], P(None, 'ka'), may hold values from -6 to 6
- grad_out: bfloat16 [32768, 1024], P('pb'), may hold values from -6 to 6
- query_blocks: int32 [128], P('pb'), may hold values from 0 to 15, as said below
Outputs:
- grad_queries: bfloat16 [32768, 1024], P(('pb', 'ka'))
- grad_keys: bfloat16 [8, 4096, 128], P('ka', 'pb')
- grad_values: bfloat16 [8, 4096, 128], P('ka', 'pb')
The draws below stay inside these ranges and needn't reach their ends.
Inputs may be any that keep to these rules, and one draw needn't show every extreme that they name: `query_blocks`: for each key and value head g, the two entries at index pb = g * 8 + l are a sequence block b and its mirror 2 * 8 - 1 - b, in either order; every block appears once among the head's entries.
All inputs are finite; a program needn't handle non-finite values.
Results may differ from the reference program's by a relative error of at most 0.0059.
Values sent between devices are 32-bit elements; how exact they have to be, the bound alone decides.
No kernel may reach another device: no remote copies, remote signals or barrier semaphores. Data moves between devices by JAX's collectives and lax.ppermute only.
A program may use at most 128 MiB of HBM per device.

```python
import jax
import jax.numpy as jnp
from jax import lax

HEADS = 8
HEAD_DIM = 128
GROUPS = 8
PB_GROUP = 8
SEQ = 4096
QBLK = 256
KBLK = 512


def draw_query_blocks(key, part):
    key = jax.random.fold_in(key, 11)
    first, second = jax.random.split(key)
    pieces = []
    for group in range(GROUPS):
        early = jax.random.permutation(jax.random.fold_in(first, group), PB_GROUP).astype(jnp.int32)
        late = 2 * PB_GROUP - 1 - early
        flips = jax.random.randint(jax.random.fold_in(second, group), (PB_GROUP,), 0, 2)
        leading = jnp.where(flips == 1, late, early)
        trailing = jnp.where(flips == 1, early, late)
        pieces.append(jnp.stack([leading, trailing], axis=1).reshape(2 * PB_GROUP))
    return jnp.concatenate(pieces).astype(jnp.int32)


def draw_queries(key, part):
    key = jax.random.fold_in(key, 21)
    first = jax.random.fold_in(key, 0)
    rows = GROUPS * SEQ
    result = jnp.clip(jax.random.normal(first, (rows, HEADS, HEAD_DIM), jnp.float32), -6.0, 6.0)
    return result.reshape(rows, HEADS * HEAD_DIM).astype(jnp.bfloat16)


def draw_keys(key, part):
    key = jax.random.fold_in(key, 31)
    result = jnp.clip(jax.random.normal(key, (GROUPS, SEQ, HEAD_DIM), jnp.float32), -6.0, 6.0)
    return result.astype(jnp.bfloat16)


def shard_levels(stream_key, dims, cuts, smallest, largest):
    def one(dim, shards_of):
        heights = jax.random.uniform(jax.random.fold_in(jax.random.fold_in(stream_key, 6), dim), (shards_of,), jnp.float32, smallest / len(cuts), largest / len(cuts))
        return jnp.repeat(jnp.exp(heights), dims[dim] // shards_of).reshape((-1,) + (1,) * (len(dims) - dim - 1))

    factor_of = one(*cuts[0])
    for cut in cuts[1:]:
        factor_of = factor_of * one(*cut)
    return factor_of


def noise(stream_key, shape, scale, limit, shards=(), kind=jnp.bfloat16):
    array = scale * jax.random.normal(stream_key, shape, jnp.float32)
    if shards:
        array = array * shard_levels(stream_key, shape, shards, -0.22, 0.18)
    return jnp.clip(array, -limit, limit).astype(kind)


def setup_inputs(seed: int = 0) -> dict:
    streams_of = jax.random.split(jax.random.key(seed), 6)
    return {
        "queries": draw_queries(jax.random.fold_in(streams_of[5], 71), 0),
        "keys": draw_keys(jax.random.fold_in(streams_of[5], 71), 0),
        "values": noise(streams_of[2], (GROUPS, SEQ, HEAD_DIM), 1.0, 6.0, ((1, 4),)),
        "grad_out": noise(streams_of[3], (GROUPS * SEQ, HEADS * HEAD_DIM), 1.0, 6.0, ((0, 64),)),
        "query_blocks": draw_query_blocks(jax.random.fold_in(streams_of[5], 71), 0),
    }


def one_head(queries, keys, values, grad_out, query_blocks):
    scale = HEAD_DIM ** -0.5
    offsets = jnp.arange(QBLK, dtype=jnp.int32)
    pos_q = (query_blocks[:, None] * QBLK + offsets[None, :]).reshape(SEQ // QBLK, QBLK)
    slots = jnp.arange(SEQ // KBLK, dtype=jnp.int32)
    owners = slots // 2
    starts = jnp.where(slots % 2 == 0, owners, SEQ // KBLK - 1 - owners)
    pos_k = (starts[:, None] * KBLK + jnp.arange(KBLK, dtype=jnp.int32)[None, :]).reshape(SEQ)
    key_wide = keys.astype(jnp.float32)
    value_wide = values.astype(jnp.float32)
    query_parts = queries.reshape(SEQ // QBLK, QBLK, HEADS, HEAD_DIM)
    grad_parts = grad_out.reshape(SEQ // QBLK, QBLK, HEADS, HEAD_DIM)

    def block_step(carry, pieces):
        key_acc, value_acc = carry
        query_part, grad_part, pos_part = pieces
        query_wide = query_part.astype(jnp.float32)
        grad_wide = grad_part.astype(jnp.float32)
        scores = jnp.einsum("qhd,kd->hqk", query_wide, key_wide) * scale
        visible = pos_k[None, None, :] <= pos_part[None, :, None]
        top = jnp.max(jnp.where(visible, scores, -1.0e30), axis=-1)
        expos = jnp.where(visible, jnp.exp(scores - top[..., None]), 0.0)
        lse = top + jnp.log(jnp.sum(expos, axis=-1))
        probs = jnp.where(visible, jnp.exp(scores - lse[..., None]), 0.0)
        slopes = jnp.einsum("qhd,kd->hqk", grad_wide, value_wide)
        delta = jnp.sum(probs * slopes, axis=-1)
        score_low = (probs * (slopes - delta[..., None]) * scale).astype(jnp.bfloat16)
        score_grads = lax.optimization_barrier(score_low).astype(jnp.float32)
        probs_low = lax.optimization_barrier(probs.astype(jnp.bfloat16)).astype(jnp.float32)
        query_grad = jnp.einsum("hqk,kd->qhd", score_grads, key_wide)
        key_acc = key_acc + jnp.einsum("hqk,qhd->kd", score_grads, query_wide)
        value_acc = value_acc + jnp.einsum("hqk,qhd->kd", probs_low, grad_wide)
        return (key_acc, value_acc), query_grad.astype(jnp.bfloat16)

    zeros = jnp.zeros((SEQ, HEAD_DIM), jnp.float32)
    (key_acc, value_acc), query_grads = lax.scan(block_step, (zeros, zeros), (query_parts, grad_parts, pos_q))
    return query_grads.reshape(SEQ, HEADS * HEAD_DIM), key_acc, value_acc


def reference(queries, keys, values, grad_out, query_blocks):
    query_list = []
    key_list = []
    value_list = []
    for group in range(GROUPS):
        rows = slice(group * SEQ, (group + 1) * SEQ)
        blocks = query_blocks[group * 2 * PB_GROUP:(group + 1) * 2 * PB_GROUP]
        query_grad, key_acc, value_acc = one_head(queries[rows], keys[group], values[group], grad_out[rows], blocks)
        query_list.append(query_grad)
        key_list.append(key_acc.reshape(SEQ // KBLK, KBLK, HEAD_DIM))
        value_list.append(value_acc.reshape(SEQ // KBLK, KBLK, HEAD_DIM))
    grad_queries = jnp.concatenate(query_list, axis=0)
    grad_keys = jnp.stack(key_list, axis=2).reshape(SEQ // KBLK, GROUPS * KBLK, HEAD_DIM).astype(jnp.bfloat16)
    grad_values = jnp.stack(value_list, axis=2).reshape(SEQ // KBLK, GROUPS * KBLK, HEAD_DIM).astype(jnp.bfloat16)
    return (grad_queries, grad_keys, grad_values)
```

```python
import functools
import math

import jax
import jax.numpy as jnp
from jax import lax
from jax.experimental import pallas as pl
from jax.experimental.pallas import tpu as pltpu
from jax.sharding import PartitionSpec as P

NEG = -1e30
HIDDEN = -2e30
TILE = 256
PAIR = 2
ZS = 8
YS = 4
F32 = jnp.float32
BF16 = jnp.bfloat16


def nt(a, b):
    return lax.dot_general(a, b, (((1,), (1,)), ((), ())), preferred_element_type=F32)


def tn(a, b):
    return lax.dot_general(a, b, (((0,), (0,)), ((), ())), preferred_element_type=F32)


def nn(a, b):
    return jnp.dot(a, b, preferred_element_type=F32)


def for_tiles(info, work):
    ka = info[2]

    def step(u, carry):
        slot = u // 4
        j = u % 4
        place = jnp.where(j < 2, 2 * ka + j, 2 * (7 - ka) + j - 2)
        block = info[slot]

        @pl.when(place < block)
        def _():
            work(slot, j, False)

        @pl.when(place == block)
        def _():
            work(slot, j, True)

        return carry

    lax.fori_loop(0, 8, step, 0)


def rows_of(index, size):
    return pl.ds(pl.multiple_of(index * size, size), size)


def visible_mask():
    shape = (TILE, TILE)
    return lax.broadcasted_iota(jnp.int32, shape, 0) <= lax.broadcasted_iota(jnp.int32, shape, 1)


def stat_kernel(width, info, q_ref, g_ref, k_ref, v_ref, out_ref, m_scr, l_scr, d_scr):
    factor = width**-0.5 * math.log2(math.e)
    heads = out_ref.shape[0] // 3
    m_scr[...] = jnp.full(m_scr.shape, NEG, F32)
    l_scr[...] = jnp.zeros(l_scr.shape, F32)
    d_scr[...] = jnp.zeros(d_scr.shape, F32)

    def work(slot, j, masked):
        keys = k_ref[0, rows_of(j, TILE), :]
        values = v_ref[0, rows_of(j, TILE), :]
        for h in range(PAIR):
            cols = slice(h * width, (h + 1) * width)
            scores = nt(keys, q_ref[rows_of(slot, TILE), cols]) * factor
            if masked:
                scores = jnp.where(visible_mask(), scores, HIDDEN)
            scores = scores.reshape(TILE // 8, 8, TILE)
            slopes = nt(values, g_ref[rows_of(slot, TILE), cols]).reshape(TILE // 8, 8, TILE)
            old = m_scr[h, slot]
            new = jnp.maximum(old, jnp.max(scores, axis=0))
            weights = jnp.exp2(scores - new[None])
            shrink = jnp.exp2(old - new)
            m_scr[h, slot] = new
            l_scr[h, slot] = l_scr[h, slot] * shrink + jnp.sum(weights, axis=0)
            d_scr[h, slot] = d_scr[h, slot] * shrink + jnp.sum(weights * slopes, axis=0)

    for_tiles(info, work)
    for h in range(PAIR):
        head = pl.program_id(0) * PAIR + h
        for slot in range(2):
            cols = slice(slot * TILE, (slot + 1) * TILE)
            m = m_scr[h, slot]
            top = jnp.max(m, axis=0, keepdims=True)
            shrink = jnp.exp2(m - top)
            out_ref[pl.ds(head, 1), cols] = top
            out_ref[pl.ds(heads + head, 1), cols] = jnp.sum(l_scr[h, slot] * shrink, axis=0, keepdims=True)
            out_ref[pl.ds(2 * heads + head, 1), cols] = jnp.sum(d_scr[h, slot] * shrink, axis=0, keepdims=True)


def grad_kernel(
    width, info, q_ref, g_ref, k_ref, v_ref, stat_ref,
    dq0, dq1, dq2, dq3, own, near_p, near_m, far_p, far_m, half_p, half_m,
    lse_scr, delta_scr, dk_scr, dv_scr, dq_scr,
):
    scale = width**-0.5
    factor = scale * math.log2(math.e)
    heads = lse_scr.shape[0]
    ka_size = stat_ref.shape[0]
    step = pl.program_id(0)

    @pl.when(step == 0)
    def _():
        top = stat_ref[0, :heads, :]
        for a in range(1, ka_size):
            top = jnp.maximum(top, stat_ref[a, :heads, :])
        total = jnp.zeros(top.shape, F32)
        dotted = jnp.zeros(top.shape, F32)
        for a in range(ka_size):
            shrink = jnp.exp2(stat_ref[a, :heads, :] - top)
            total += stat_ref[a, heads : 2 * heads, :] * shrink
            dotted += stat_ref[a, 2 * heads :, :] * shrink
        lse_scr[...] = top + jnp.log2(total)
        delta_scr[...] = dotted / total
        dk_scr[...] = jnp.zeros(dk_scr.shape, F32)
        dv_scr[...] = jnp.zeros(dv_scr.shape, F32)

    dq_scr[...] = jnp.zeros(dq_scr.shape, F32)

    def work(slot, j, masked):
        keys = k_ref[0, rows_of(j, TILE), :]
        values = v_ref[0, rows_of(j, TILE), :]
        key_sum = dk_scr[rows_of(j, TILE), :]
        value_sum = dv_scr[rows_of(j, TILE), :]
        for h in range(PAIR):
            cols = slice(h * width, (h + 1) * width)
            head = step * PAIR + h
            q = q_ref[rows_of(slot, TILE), cols]
            g = g_ref[rows_of(slot, TILE), cols]
            lse = lse_scr[pl.ds(head, 1), rows_of(slot, TILE)]
            delta = delta_scr[pl.ds(head, 1), rows_of(slot, TILE)]
            probs = jnp.exp2(nt(keys, q) * factor - lse)
            if masked:
                probs = jnp.where(visible_mask(), probs, 0.0)
            slopes = nt(values, g)
            score_grads = (probs * (slopes - delta) * scale).astype(BF16)
            value_sum += nn(probs.astype(BF16), g)
            key_sum += nn(score_grads, q)
            dq_scr[rows_of(slot, TILE), cols] += tn(score_grads, keys)
        dk_scr[rows_of(j, TILE), :] = key_sum
        dv_scr[rows_of(j, TILE), :] = value_sum

    for_tiles(info, work)

    ka = info[2]
    for rel, out in enumerate((dq0, dq1, dq2, dq3)):
        share = jnp.bitwise_xor(ka, rel)
        out[...] = dq_scr[rows_of(share, dq0.shape[0]), :]

    @pl.when(step == pl.num_programs(0) - 1)
    def _():
        z = info[4]

        def put(out, at, rel, pieces):
            for g in pieces:
                row = lax.rem(z + rel, ZS) * 8 + g * 8 * ZS
                for kv, acc in enumerate((dk_scr, dv_scr)):
                    for blk in range(2):
                        start = pl.multiple_of(row + blk * (dk_scr.shape[0] // 2), 8)
                        out[at : at + 8, :] = acc[pl.ds(start, 8), :]
                        at += 8

        every = range(8)
        put(own, 0, 0, every)
        put(near_p, 0, 1, every)
        put(near_p, 256, 3, every)
        put(near_m, 0, 7, every)
        put(near_m, 256, 5, every)
        put(far_p, 0, 2, every)
        put(far_m, 0, 6, every)
        put(half_p, 0, 4, range(4))
        put(half_m, 0, 4, range(4, 8))


def sum_kernel(info, own, near_p, near_m, far_p, far_m, mine, other):
    xh, y = info[5], info[6]
    for out, there in ((mine, xh), (other, 1 - xh)):
        for rel in range(YS):
            start = rows_of(there * YS + lax.rem(y + rel, YS), 32)
            out[rel] = (own[start, :] + near_p[start, :] + near_m[start, :]) + (far_p[start, :] + far_m[start, :])


def place_kernel(info, mine, other, from1, from2, from3, dk_ref, dv_ref, scr):
    xh, y = info[5], info[6]
    parts = [(0, mine[0], other[0])]
    parts += [(rel, ref[0], ref[1]) for rel, ref in ((1, from1), (2, from2), (3, from3))]
    for rel, near, far in parts:
        from_y = lax.rem(y + YS - rel, YS)
        for part, from_x in ((near, xh), (far, 1 - xh)):
            head = from_x * YS + from_y
            for kv in range(2):
                for blk in range(2):
                    at = (kv * 2 + blk) * 8
                    scr[kv, blk, :, pl.ds(head, 1), :] = part[at : at + 8, :].reshape(8, 1, part.shape[1])
    for kv, out in enumerate((dk_ref, dv_ref)):
        for blk in range(2):
            out[blk] = scr[kv, blk].reshape(64, out.shape[2]).astype(BF16)


def on_device(queries, keys, values, grad_out, query_blocks):
    head_count, key_count, width = keys.shape
    query_count = queries.shape[0]
    heads = queries.shape[1] // width
    pb = lax.axis_index("pb")
    ka = lax.axis_index("ka")
    pb_size = lax.axis_size("pb")
    owner = pb // ZS
    info = jnp.stack(
        [query_blocks[0], query_blocks[1], ka, owner, pb % ZS, owner // YS, owner % YS]
    ).astype(jnp.int32)
    steps = heads // PAIR

    part = pl.BlockSpec((query_count, PAIR * width), lambda i, s: (0, i))
    whole = pl.BlockSpec((1, key_count, width), lambda i, s: (s[3], 0, 0))
    params = pltpu.CompilerParams(vmem_limit_bytes=48 * 2**20)

    def fixed(shape):
        return pl.BlockSpec(shape, lambda i, s: (0,) * len(shape))

    def array(shape, dtype=F32):
        return jax.ShapeDtypeStruct(shape, dtype)

    stats = pl.pallas_call(
        functools.partial(stat_kernel, width),
        out_shape=array((3 * heads, query_count)),
        grid_spec=pltpu.PrefetchScalarGridSpec(
            num_scalar_prefetch=1,
            grid=(steps,),
            in_specs=[part, part, whole, whole],
            out_specs=fixed((3 * heads, query_count)),
            scratch_shapes=[pltpu.VMEM((PAIR, 2, 8, TILE), F32)] * 3,
        ),
        compiler_params=params,
        name="row_stats",
    )(info, queries, grad_out, keys, values)
    gathered = lax.all_gather(stats, "ka")

    share = query_count // 4
    chunk = (256, width)
    shapes = [chunk, (512, width), (512, width), chunk, chunk, (128, width), (128, width)]
    outs = pl.pallas_call(
        functools.partial(grad_kernel, width),
        out_shape=[array((share, heads * width))] * 4 + [array(s) for s in shapes],
        grid_spec=pltpu.PrefetchScalarGridSpec(
            num_scalar_prefetch=1,
            grid=(steps,),
            in_specs=[part, part, whole, whole, fixed(gathered.shape)],
            out_specs=[pl.BlockSpec((share, PAIR * width), lambda i, s: (0, i))] * 4 + [fixed(s) for s in shapes],
            scratch_shapes=[
                pltpu.VMEM((heads, query_count), F32),
                pltpu.VMEM((heads, query_count), F32),
                pltpu.VMEM((key_count, width), F32),
                pltpu.VMEM((key_count, width), F32),
                pltpu.VMEM((query_count, PAIR * width), F32),
            ],
        ),
        compiler_params=params,
        name="grads",
    )(info, queries, grad_out, keys, values, gathered)
    dq0, dq1, dq2, dq3, own, near_p, near_m, far_p, far_m, half_p, half_m = outs

    def along_z(x, by):
        return lax.ppermute(x, "pb", [(p, p // ZS * ZS + (p + by) % ZS) for p in range(pb_size)])

    def along_y(x, by):
        return lax.ppermute(
            x, "pb", [(p, (p // (ZS * YS) * YS + (p // ZS + by) % YS) * ZS + p % ZS) for p in range(pb_size)]
        )

    def across_x(x):
        return lax.ppermute(x, "pb", [(p, (p + pb_size // 2) % pb_size) for p in range(pb_size)])

    def across_ka(x, by):
        return lax.ppermute(x, "ka", [(a, a ^ by) for a in range(4)])

    got_np = along_z(near_p, 1)
    got_nm = along_z(near_m, ZS - 1)
    got_hp = along_z(half_p, 2)
    got_hm = along_z(half_m, ZS - 2)

    got3 = across_ka(dq3, 1)
    for_other = dq2 + got3
    got1 = across_ka(dq1, 1)
    got2 = across_ka(for_other, 2)

    far_p = far_p + got_np[256:] + jnp.pad(got_hp, ((0, 128), (0, 0)))
    far_m = far_m + got_nm[256:] + jnp.pad(got_hm, ((128, 0), (0, 0)))
    got_fp = along_z(far_p, 2)
    got_fm = along_z(far_m, ZS - 2)

    small = pl.BlockSpec(memory_space=pltpu.VMEM)
    scalars = pl.BlockSpec(memory_space=pltpu.SMEM)
    mine, other = pl.pallas_call(
        sum_kernel,
        out_shape=[array((YS, 32, width))] * 2,
        in_specs=[scalars] + [small] * 5,
        out_specs=[small] * 2,
        name="add_parts",
    )(info, own, got_np[:256], got_nm[:256], got_fp, got_fm)
    other = across_x(other)
    pairs = [jnp.stack([mine[k], other[k]]) for k in range(1, YS)]
    got_y = [along_y(x, k) for k, x in zip((2, 1, 3), (pairs[1], pairs[0], pairs[2]))]
    grad_keys, grad_values = pl.pallas_call(
        place_kernel,
        out_shape=[array((2, 64, width), BF16)] * 2,
        in_specs=[scalars] + [small] * 5,
        out_specs=[small] * 2,
        scratch_shapes=[pltpu.VMEM((2, 2, 8, 8, width), F32)],
        name="place_rows",
    )(info, mine, other, got_y[1], got_y[0], got_y[2])

    grad_queries = (dq0 + got1 + got2).astype(BF16)
    return grad_queries, grad_keys, grad_values


def solution(mesh):
    placed = (P("pb", None), P(None, "ka", None), P(None, "ka", None), P("pb", None), P("pb"))
    return jax.shard_map(
        on_device,
        mesh=mesh,
        in_specs=placed,
        out_specs=(P(("pb", "ka"), None), P("ka", "pb", None), P("ka", "pb", None)),
        check_vma=False,
    )
```

```python
import functools
import math

import jax
import jax.numpy as jnp
from jax import lax
from jax.experimental import pallas as pl
from jax.experimental.pallas import tpu as pltpu
from jax.sharding import PartitionSpec as P

NEG = -1e30
HIDDEN = -2e30
TILE = 256
GROUP = 4
ZS = 8
YS = 4
F32 = jnp.float32
BF16 = jnp.bfloat16


def nt(a, b):
    return lax.dot_general(a, b, (((1,), (1,)), ((), ())), preferred_element_type=F32)


def nn(a, b):
    return jnp.dot(a, b, preferred_element_type=F32)


def for_tiles(info, work):
    ka = info[2]

    def step(u, carry):
        slot = u // 4
        j = u % 4
        place = jnp.where(j < 2, 2 * ka + j, 2 * (7 - ka) + j - 2)
        block = info[slot]

        @pl.when(place < block)
        def _():
            work(slot, j, False)

        @pl.when(place == block)
        def _():
            work(slot, j, True)

        return carry

    lax.fori_loop(0, 8, step, 0)


def rows_of(index, size):
    return pl.ds(pl.multiple_of(index * size, size), size)


def visible_mask():
    shape = (TILE, TILE)
    return lax.broadcasted_iota(jnp.int32, shape, 0) <= lax.broadcasted_iota(jnp.int32, shape, 1)


def load(pairs, sems):
    copies = [pltpu.make_async_copy(src, dst, sems.at[i]) for i, (src, dst) in enumerate(pairs)]
    for copy in copies:
        copy.start()
    for copy in copies:
        copy.wait()


def stat_kernel(
    width, info, q_hbm, g_hbm, k_hbm, v_hbm, out_ref, q_ref, g_ref, k_ref, v_ref, m_scr, l_scr, d_scr, sems
):
    load([(k_hbm.at[info[3]], k_ref), (q_hbm, q_ref), (v_hbm.at[info[3]], v_ref), (g_hbm, g_ref)], sems)
    factor = width**-0.5 * math.log2(math.e)
    heads = out_ref.shape[0] // 3
    m_scr[...] = jnp.full(m_scr.shape, NEG, F32)
    l_scr[...] = jnp.zeros(l_scr.shape, F32)
    d_scr[...] = jnp.zeros(d_scr.shape, F32)
    def work(slot, j, masked):
        keys = k_ref[rows_of(j, TILE), :]
        values = v_ref[rows_of(j, TILE), :]
        for h in range(heads):
            cols = slice(h * width, (h + 1) * width)
            scores = nt(keys, q_ref[rows_of(slot, TILE), cols]) * factor
            if masked:
                scores = jnp.where(visible_mask(), scores, HIDDEN)
            scores = scores.reshape(TILE // 8, 8, TILE)
            slopes = nt(values, g_ref[rows_of(slot, TILE), cols]).reshape(TILE // 8, 8, TILE)
            old = m_scr[h, slot]
            new = jnp.maximum(old, jnp.max(scores, axis=0))
            weights = jnp.exp2(scores - new[None])
            shrink = jnp.exp2(old - new)
            m_scr[h, slot] = new
            l_scr[h, slot] = l_scr[h, slot] * shrink + jnp.sum(weights, axis=0)
            d_scr[h, slot] = d_scr[h, slot] * shrink + jnp.sum(weights * slopes, axis=0)
    for_tiles(info, work)
    for h in range(heads):
        for slot in range(2):
            cols = slice(slot * TILE, (slot + 1) * TILE)
            m = m_scr[h, slot]
            top = jnp.max(m, axis=0, keepdims=True)
            shrink = jnp.exp2(m - top)
            out_ref[h : h + 1, cols] = top
            out_ref[heads + h : heads + h + 1, cols] = jnp.sum(l_scr[h, slot] * shrink, axis=0, keepdims=True)
            out_ref[2 * heads + h : 2 * heads + h + 1, cols] = jnp.sum(d_scr[h, slot] * shrink, axis=0, keepdims=True)


def grad_kernel(
    width, info, q_hbm, g_hbm, k_hbm, v_hbm, stat_ref,
    dq0, dq1, dq2, dq3, own, near_p, near_m, far_p, far_m, half_p, half_m,
    q_ref, g_ref, k_ref, v_ref, qt_ref, gt_ref, kt_ref, lse_scr, delta_scr, dk_scr, dv_scr, dq_scr,
    dk_rows, dv_rows, sems,
):
    load([(k_hbm.at[info[3]], k_ref), (q_hbm, q_ref), (v_hbm.at[info[3]], v_ref), (g_hbm, g_ref)], sems)
    scale = width**-0.5
    factor = scale * math.log2(math.e)
    heads = lse_scr.shape[0]
    ka_size = stat_ref.shape[0]
    top = stat_ref[0, :heads, :]
    for a in range(1, ka_size):
        top = jnp.maximum(top, stat_ref[a, :heads, :])
    total = jnp.zeros(top.shape, F32)
    dotted = jnp.zeros(top.shape, F32)
    for a in range(ka_size):
        shrink = jnp.exp2(stat_ref[a, :heads, :] - top)
        total += stat_ref[a, heads : 2 * heads, :] * shrink
        dotted += stat_ref[a, 2 * heads :, :] * shrink
    lse_scr[...] = top + jnp.log2(total)
    delta_scr[...] = dotted / total
    dk_scr[...] = jnp.zeros(dk_scr.shape, F32)
    dv_scr[...] = jnp.zeros(dv_scr.shape, F32)
    dq_scr[...] = jnp.zeros(dq_scr.shape, F32)
    for slot in range(2):
        for h in range(heads):
            at = (slot * heads + h) * TILE
            qt_ref[:, at:at + TILE] = q_ref[slot * TILE:(slot + 1) * TILE, h * width:(h + 1) * width].T
            gt_ref[:, at:at + TILE] = g_ref[slot * TILE:(slot + 1) * TILE, h * width:(h + 1) * width].T
    kt_ref[...] = k_ref[...].T

    def work(slot, j, masked):
        keys = k_ref[rows_of(j, TILE), :]
        values = v_ref[rows_of(j, TILE), :]
        kt = kt_ref[:, rows_of(j, TILE)]
        span = GROUP * TILE
        for first in range(0, heads, GROUP):
            at = pl.ds(pl.multiple_of(slot * heads * TILE + first * TILE, TILE), span)
            qt = qt_ref[:, at]
            gt = gt_ref[:, at]
            lows, grads = [], []
            for i in range(GROUP):
                h = first + i
                part = slice(i * TILE, (i + 1) * TILE)
                lse = lse_scr[h : h + 1, rows_of(slot, TILE)]
                delta = delta_scr[h : h + 1, rows_of(slot, TILE)]
                probs = jnp.exp2(nn(keys, qt[:, part]) * factor - lse)
                if masked:
                    probs = jnp.where(visible_mask(), probs, 0.0)
                slopes = nn(values, gt[:, part])
                grads.append((probs * (slopes - delta) * scale).astype(BF16))
                lows.append(probs.astype(BF16))
            low = jnp.concatenate(lows, axis=1)
            grad = jnp.concatenate(grads, axis=1)
            dv_scr[:, rows_of(j, TILE)] += nt(gt, low)
            dk_scr[:, rows_of(j, TILE)] += nt(qt, grad)
            dq_scr[:, at] += nn(kt, grad)
    for_tiles(info, work)

    ka = info[2]
    half = TILE // 2
    for rel, out in enumerate((dq0, dq1, dq2, dq3)):
        share = jnp.bitwise_xor(ka, rel)
        slot, side = share // 2, share % 2
        for h in range(heads):
            start = pl.multiple_of((slot * heads + h) * TILE + side * half, half)
            out[:, h * half:(h + 1) * half] = dq_scr[:, pl.ds(start, half)]
    z = info[4]
    dk_rows[...] = dk_scr[...].T
    dv_rows[...] = dv_scr[...].T

    def put(out, at, rel, pieces):
        for g in pieces:
            row = lax.rem(z + rel, ZS) * 8 + g * 8 * ZS
            for kv, acc in enumerate((dk_rows, dv_rows)):
                for blk in range(2):
                    start = pl.multiple_of(row + blk * (dk_rows.shape[0] // 2), 8)
                    out[at : at + 8, :] = acc[pl.ds(start, 8), :]
                    at += 8

    every = range(8)
    put(own, 0, 0, every)
    put(near_p, 0, 1, every)
    put(near_p, 256, 3, every)
    put(near_m, 0, 7, every)
    put(near_m, 256, 5, every)
    put(far_p, 0, 2, every)
    put(far_m, 0, 6, every)
    put(half_p, 0, 4, range(4))
    put(half_m, 0, 4, range(4, 8))


def sum_kernel(info, own, near_p, near_m, far_p, far_m, mine, other):
    xh, y = info[5], info[6]
    for out, there in ((mine, xh), (other, 1 - xh)):
        for rel in range(YS):
            start = rows_of(there * YS + lax.rem(y + rel, YS), 32)
            out[rel] = (own[start, :] + near_p[start, :] + near_m[start, :]) + (far_p[start, :] + far_m[start, :])


def place_kernel(info, mine, other, from1, from2, from3, dk_ref, dv_ref, scr):
    xh, y = info[5], info[6]
    parts = [(0, mine[0], other[0])]
    parts += [(rel, ref[0], ref[1]) for rel, ref in ((1, from1), (2, from2), (3, from3))]
    for rel, near, far in parts:
        from_y = lax.rem(y + YS - rel, YS)
        for part, from_x in ((near, xh), (far, 1 - xh)):
            head = from_x * YS + from_y
            for kv in range(2):
                for blk in range(2):
                    at = (kv * 2 + blk) * 8
                    scr[kv, blk, :, pl.ds(head, 1), :] = part[at : at + 8, :].reshape(8, 1, part.shape[1])
    for kv, out in enumerate((dk_ref, dv_ref)):
        for blk in range(2):
            out[blk] = scr[kv, blk].reshape(64, out.shape[2]).astype(BF16)


def query_kernel(a_ref, b_ref, c_ref, out_ref):
    rows, width = out_ref.shape[0], a_ref.shape[0]
    for h in range(out_ref.shape[1] // width):
        part = slice(h * rows, (h + 1) * rows)
        total = a_ref[:, part] + b_ref[:, part] + c_ref[:, part]
        out_ref[:, h * width : (h + 1) * width] = total.T.astype(BF16)


def array(shape, dtype=F32):
    return jax.ShapeDtypeStruct(shape, dtype)


SMALL = pl.BlockSpec(memory_space=pltpu.VMEM)
SCALARS = pl.BlockSpec(memory_space=pltpu.SMEM)
LARGE = pl.BlockSpec(memory_space=pltpu.HBM)
PARAMS = pltpu.CompilerParams(vmem_limit_bytes=40 * 2**20)


def row_stats(info, queries, grad_out, keys, values):
    _, key_count, width = keys.shape
    query_count = queries.shape[0]
    heads = queries.shape[1] // width
    return pl.pallas_call(
        functools.partial(stat_kernel, width),
        out_shape=array((3 * heads, query_count)),
        in_specs=[SCALARS] + [LARGE] * 4,
        out_specs=SMALL,
        scratch_shapes=[pltpu.VMEM(queries.shape, BF16)] * 2
        + [pltpu.VMEM((key_count, width), BF16)] * 2
        + [pltpu.VMEM((heads, 2, 8, TILE), F32)] * 3
        + [pltpu.SemaphoreType.DMA((4,))],
        compiler_params=PARAMS,
        name="row_stats",
    )(info, queries, grad_out, keys, values)


def gradients(info, queries, grad_out, keys, values, gathered):
    _, key_count, width = keys.shape
    query_count = queries.shape[0]
    heads = queries.shape[1] // width
    share = query_count // 4
    chunk = (256, width)
    shapes = [chunk, (512, width), (512, width), chunk, chunk, (128, width), (128, width)]
    return pl.pallas_call(
        functools.partial(grad_kernel, width),
        out_shape=[array((width, heads * share))] * 4 + [array(s) for s in shapes],
        in_specs=[SCALARS] + [LARGE] * 4 + [SMALL],
        out_specs=[SMALL] * 11,
        scratch_shapes=[pltpu.VMEM(queries.shape, BF16)] * 2
        + [pltpu.VMEM((key_count, width), BF16)] * 2
        + [pltpu.VMEM((width, query_count * heads), BF16)] * 2
        + [pltpu.VMEM((width, key_count), BF16)]
        + [pltpu.VMEM((heads, query_count), F32)] * 2
        + [pltpu.VMEM((width, key_count), F32)] * 2
        + [pltpu.VMEM((width, query_count * heads), F32)]
        + [pltpu.VMEM((key_count, width), F32)] * 2
        + [pltpu.SemaphoreType.DMA((4,))],
        compiler_params=PARAMS,
        name="grads",
    )(info, queries, grad_out, keys, values, gathered)


def on_device(queries, keys, values, grad_out, query_blocks):
    width = keys.shape[2]
    query_count = queries.shape[0]
    pb = lax.axis_index("pb")
    ka = lax.axis_index("ka")
    pb_size = lax.axis_size("pb")
    owner = pb // ZS
    info = jnp.stack(
        [query_blocks[0], query_blocks[1], ka, owner, pb % ZS, owner // YS, owner % YS]
    ).astype(jnp.int32)
    stats = row_stats(info, queries, grad_out, keys, values)
    gathered = lax.all_gather(stats, "ka")

    outs = gradients(info, queries, grad_out, keys, values, gathered)
    dq0, dq1, dq2, dq3, own, near_p, near_m, far_p, far_m, half_p, half_m = outs

    def along_z(x, by):
        return lax.ppermute(x, "pb", [(p, p // ZS * ZS + (p + by) % ZS) for p in range(pb_size)])

    def along_y(x, by):
        return lax.ppermute(
            x, "pb", [(p, (p // (ZS * YS) * YS + (p // ZS + by) % YS) * ZS + p % ZS) for p in range(pb_size)]
        )

    def across_x(x):
        return lax.ppermute(x, "pb", [(p, (p + pb_size // 2) % pb_size) for p in range(pb_size)])

    def across_ka(x, by):
        return lax.ppermute(x, "ka", [(a, a ^ by) for a in range(4)])

    got_np = along_z(near_p, 1)
    got_nm = along_z(near_m, ZS - 1)
    got_hp = along_z(half_p, 2)
    got_hm = along_z(half_m, ZS - 2)

    got3 = across_ka(dq3, 1)
    for_other = dq2 + got3
    got1 = across_ka(dq1, 1)
    got2 = across_ka(for_other, 2)

    far_p = far_p + got_np[256:] + jnp.pad(got_hp, ((0, 128), (0, 0)))
    far_m = far_m + got_nm[256:] + jnp.pad(got_hm, ((128, 0), (0, 0)))
    got_fp = along_z(far_p, 2)
    got_fm = along_z(far_m, ZS - 2)

    mine, other = pl.pallas_call(
        sum_kernel,
        out_shape=[array((YS, 32, width))] * 2,
        in_specs=[SCALARS] + [SMALL] * 5,
        out_specs=[SMALL] * 2,
        name="add_parts",
    )(info, own, got_np[:256], got_nm[:256], got_fp, got_fm)
    other = across_x(other)
    pairs = [jnp.stack([mine[k], other[k]]) for k in range(1, YS)]
    got_y = [along_y(x, k) for k, x in zip((2, 1, 3), (pairs[1], pairs[0], pairs[2]))]
    grad_keys, grad_values = pl.pallas_call(
        place_kernel,
        out_shape=[array((2, 64, width), BF16)] * 2,
        in_specs=[SCALARS] + [SMALL] * 5,
        out_specs=[SMALL] * 2,
        scratch_shapes=[pltpu.VMEM((2, 2, 8, 8, width), F32)],
        name="place_rows",
    )(info, mine, other, got_y[1], got_y[0], got_y[2])

    grad_queries = pl.pallas_call(
        query_kernel,
        out_shape=array((query_count // 4, queries.shape[1]), BF16),
        in_specs=[SMALL] * 3,
        out_specs=SMALL,
        name="finish_queries",
    )(dq0, got1, got2)
    return grad_queries, grad_keys, grad_values


def solution(mesh):
    placed = (P("pb", None), P(None, "ka", None), P(None, "ka", None), P("pb", None), P("pb"))
    return jax.shard_map(
        on_device,
        mesh=mesh,
        in_specs=placed,
        out_specs=(P(("pb", "ka"), None), P("ka", "pb", None), P("ka", "pb", None)),
        check_vma=False,
    )
```

```python
import functools
import math

import jax
import jax.numpy as jnp
from jax import lax
from jax.experimental import pallas as pl
from jax.experimental.pallas import tpu as pltpu
from jax.sharding import PartitionSpec as P

NEG = -1e30
HIDDEN = -2e30
TILE = 256
GROUP = 8
ZS = 8
YS = 4
F32 = jnp.float32
BF16 = jnp.bfloat16


def nt(a, b):
    return lax.dot_general(a, b, (((1,), (1,)), ((), ())), preferred_element_type=F32)


def nn(a, b):
    return jnp.dot(a, b, preferred_element_type=F32)


def own_head():
    return lax.axis_index("pb") // ZS


def own_z():
    return lax.axis_index("pb") % ZS


def for_tiles(blocks, work, before_slot=None):
    ka = lax.axis_index("ka")

    def step(u, n):
        slot = u // 4
        j = u % 4
        place = jnp.where(j < 2, 2 * ka + j, 2 * (7 - ka) + j - 2)
        block = blocks[slot]
        if before_slot is not None:
            pl.when(u == 4)(functools.partial(before_slot, 1))

        @pl.when(place < block)
        def _():
            work(slot, j, False, n)

        @pl.when(place == block)
        def _():
            work(slot, j, True, n)

        return n + jnp.where(place <= block, 1, 0)

    if before_slot is not None:
        before_slot(0)
    lax.fori_loop(0, 8, step, 0)


def rows_of(index, size):
    return pl.ds(pl.multiple_of(index * size, size), size)


def visible_mask():
    shape = (TILE, TILE)
    return lax.broadcasted_iota(jnp.int32, shape, 0) <= lax.broadcasted_iota(jnp.int32, shape, 1)


def stat_kernel(
    width, blocks, q_hbm, g_hbm, k_hbm, v_hbm,
    out_ref, qt_ref, gt_ref, k_ref, v_ref, kt_ref,
    q_ref, g_ref, m_scr, l_scr, d_scr, sems,
):
    def slot_rows(slot):
        return slice(slot * TILE, (slot + 1) * TILE)

    head = own_head()
    copies = [
        pltpu.make_async_copy(k_hbm.at[head], k_ref, sems.at[0]),
        pltpu.make_async_copy(v_hbm.at[head], v_ref, sems.at[1]),
    ]
    for slot in range(2):
        rows = slot_rows(slot)
        copies.append(pltpu.make_async_copy(q_hbm.at[rows], q_ref.at[rows], sems.at[2 + 2 * slot]))
        copies.append(pltpu.make_async_copy(g_hbm.at[rows], g_ref.at[rows], sems.at[3 + 2 * slot]))
    for copy in copies:
        copy.start()
    factor = width**-0.5 * math.log2(math.e)
    heads = out_ref.shape[0] // 3
    m_scr[...] = jnp.full(m_scr.shape, NEG, F32)
    l_scr[...] = jnp.zeros(l_scr.shape, F32)
    d_scr[...] = jnp.zeros(d_scr.shape, F32)

    def before_slot(slot):
        if slot == 0:
            for copy in copies[:2]:
                copy.wait()
            kt_ref[...] = k_ref[...].T
        for copy in copies[2 + 2 * slot : 4 + 2 * slot]:
            copy.wait()
        for h in range(heads):
            cols = slice(h * width, (h + 1) * width)
            at = (slot * heads + h) * TILE
            qt_ref[:, at : at + TILE] = q_ref[slot_rows(slot), cols].T
            gt_ref[:, at : at + TILE] = g_ref[slot_rows(slot), cols].T

    def work(slot, j, masked, n):
        keys = k_ref[rows_of(j, TILE), :]
        values = v_ref[rows_of(j, TILE), :]
        for h in range(heads):
            at = rows_of(slot * heads + h, TILE)
            scores = nn(keys, qt_ref[:, at]) * factor
            if masked:
                scores = jnp.where(visible_mask(), scores, HIDDEN)
            scores = scores.reshape(TILE // 8, 8, TILE)
            slopes = nn(values, gt_ref[:, at]).reshape(TILE // 8, 8, TILE)
            old = m_scr[h, slot]
            new = jnp.maximum(old, jnp.max(scores, axis=0))
            weights = jnp.exp2(scores - new[None])
            shrink = jnp.exp2(old - new)
            m_scr[h, slot] = new
            l_scr[h, slot] = l_scr[h, slot] * shrink + jnp.sum(weights, axis=0)
            d_scr[h, slot] = d_scr[h, slot] * shrink + jnp.sum(weights * slopes, axis=0)

    for_tiles(blocks, work, before_slot)
    for h in range(heads):
        for slot in range(2):
            cols = slot_rows(slot)
            m = m_scr[h, slot]
            top = jnp.max(m, axis=0, keepdims=True)
            shrink = jnp.exp2(m - top)
            out_ref[h : h + 1, cols] = top
            out_ref[heads + h : heads + h + 1, cols] = jnp.sum(l_scr[h, slot] * shrink, axis=0, keepdims=True)
            out_ref[2 * heads + h : 2 * heads + h + 1, cols] = jnp.sum(d_scr[h, slot] * shrink, axis=0, keepdims=True)


def grad_kernel(
    width, blocks, qt_ref, gt_ref, k_ref, v_ref, kt_ref, stat_ref,
    dq0, dq1, dq2, dq3, own, near_p, near_m, far_p, far_m, half_p, half_m,
    lse_scr, delta_scr, dk_scr, dv_scr, dk_rows, dv_rows, dq_scr,
):
    scale = width**-0.5
    factor = scale * math.log2(math.e)
    heads = lse_scr.shape[0]
    ka_size = stat_ref.shape[0]
    top = stat_ref[0, :heads, :]
    for a in range(1, ka_size):
        top = jnp.maximum(top, stat_ref[a, :heads, :])
    total = jnp.zeros(top.shape, F32)
    dotted = jnp.zeros(top.shape, F32)
    for a in range(ka_size):
        shrink = jnp.exp2(stat_ref[a, :heads, :] - top)
        total += stat_ref[a, heads : 2 * heads, :] * shrink
        dotted += stat_ref[a, 2 * heads :, :] * shrink
    lse_scr[...] = top + jnp.log2(total)
    delta_scr[...] = dotted / total
    dk_scr[...] = jnp.zeros(dk_scr.shape, F32)
    dv_scr[...] = jnp.zeros(dv_scr.shape, F32)
    dq_scr[...] = jnp.zeros(dq_scr.shape, F32)

    def work(slot, j, masked, n):
        kt = kt_ref[:, rows_of(j, TILE)]
        keys = k_ref[rows_of(j, TILE), :]
        values = v_ref[rows_of(j, TILE), :]
        span = GROUP * TILE
        for first in range(0, heads, GROUP):
            at = pl.ds(pl.multiple_of((slot * heads + first) * TILE, TILE), span)
            qt = qt_ref[:, at]
            gt = gt_ref[:, at]
            lows, grads = [], []
            for i in range(GROUP):
                h = first + i
                part = slice(i * TILE, (i + 1) * TILE)
                lse = lse_scr[h : h + 1, rows_of(slot, TILE)]
                delta = delta_scr[h : h + 1, rows_of(slot, TILE)]
                probs = jnp.exp2(nn(keys, qt[:, part]) * factor - lse)
                if masked:
                    probs = jnp.where(visible_mask(), probs, 0.0)
                slopes = nn(values, gt[:, part])
                grads.append((probs * (slopes - delta) * scale).astype(BF16))
                lows.append(probs.astype(BF16))
            low = jnp.concatenate(lows, axis=1)
            grad = jnp.concatenate(grads, axis=1)
            dq_scr[:, at] += nn(kt, grad)
            dv_scr[:, rows_of(j, TILE)] += nt(gt, low)
            dk_scr[:, rows_of(j, TILE)] += nt(qt, grad)

    for_tiles(blocks, work)

    ka = lax.axis_index("ka")
    half = TILE // 2
    for rel, out in enumerate((dq0, dq1, dq2, dq3)):
        share = jnp.bitwise_xor(ka, rel)
        slot, side = share // 2, share % 2
        for h in range(heads):
            start = pl.multiple_of((slot * heads + h) * TILE + side * half, half)
            out[:, h * half : (h + 1) * half] = dq_scr[:, pl.ds(start, half)]

    z = own_z()
    dk_rows[...] = dk_scr[...].T
    dv_rows[...] = dv_scr[...].T

    def put(out, at, rel, pieces):
        for g in pieces:
            row = lax.rem(z + rel, ZS) * 8 + g * 8 * ZS
            for acc in (dk_rows, dv_rows):
                for blk in range(2):
                    start = pl.multiple_of(row + blk * (dk_rows.shape[0] // 2), 8)
                    out[at : at + 8, :] = acc[pl.ds(start, 8), :]
                    at += 8

    every = range(8)
    put(own, 0, 0, every)
    put(near_p, 0, 1, every)
    put(near_p, 256, 3, every)
    put(near_m, 0, 7, every)
    put(near_m, 256, 5, every)
    put(far_p, 0, 2, every)
    put(far_m, 0, 6, every)
    put(half_p, 0, 4, range(4))
    put(half_m, 0, 4, range(4, 8))


def merge_kernel(far_p, got_np, got_hp, far_m, got_nm, got_hm, dq, got_dq, out_p, out_m, out_dq):
    out_dq[...] = dq[...] + got_dq[...]
    half = got_hp.shape[0]
    out_p[:half] = far_p[:half] + got_np[2 * half :][:half] + got_hp[...]
    out_p[half:] = far_p[half:] + got_np[3 * half :]
    out_m[:half] = far_m[:half] + got_nm[2 * half :][:half]
    out_m[half:] = far_m[half:] + got_nm[3 * half :] + got_hm[...]


def sum_kernel(own, near_p, near_m, far_p, far_m, out):
    rows = own.shape[0]
    out[...] = (own[...] + near_p[:rows] + near_m[:rows]) + (far_p[...] + far_m[...])


def place_kernel(parts, dk_ref, dv_ref, scr):
    for head in range(parts.shape[0] // 32):
        for kv in range(2):
            for blk in range(2):
                at = head * 32 + (kv * 2 + blk) * 8
                scr[kv, blk, :, head : head + 1, :] = parts[at : at + 8, :].reshape(8, 1, parts.shape[1])
    for kv, out in enumerate((dk_ref, dv_ref)):
        for blk in range(2):
            out[blk] = scr[kv, blk].reshape(64, out.shape[2]).astype(BF16)


def query_kernel(a_ref, b_ref, c_ref, out_ref):
    rows, width = out_ref.shape[0], a_ref.shape[0]
    for h in range(out_ref.shape[1] // width):
        part = slice(h * rows, (h + 1) * rows)
        total = a_ref[:, part] + b_ref[:, part] + c_ref[:, part]
        out_ref[:, h * width : (h + 1) * width] = total.T.astype(BF16)


def array(shape, dtype=F32):
    return jax.ShapeDtypeStruct(shape, dtype)


SMALL = pl.BlockSpec(memory_space=pltpu.VMEM)
SCALARS = pl.BlockSpec(memory_space=pltpu.SMEM)
LARGE = pl.BlockSpec(memory_space=pltpu.HBM)


def vmem(mib):
    return pltpu.CompilerParams(vmem_limit_bytes=int(mib * 2**20))


def row_stats(blocks, queries, grad_out, keys, values):
    _, key_count, width = keys.shape
    query_count = queries.shape[0]
    heads = queries.shape[1] // width
    turned = array((width, query_count * heads), BF16)
    own = array((key_count, width), BF16)
    return pl.pallas_call(
        functools.partial(stat_kernel, width),
        out_shape=[array((3 * heads, query_count)), turned, turned, own, own, array((width, key_count), BF16)],
        in_specs=[SCALARS] + [LARGE] * 4,
        out_specs=[SMALL] * 6,
        scratch_shapes=[pltpu.VMEM(queries.shape, BF16)] * 2
        + [pltpu.VMEM((heads, 2, 8, TILE), F32)] * 3
        + [pltpu.SemaphoreType.DMA((6,))],
        compiler_params=vmem(24),
        name="row_stats",
    )(blocks, queries, grad_out, keys, values)


def gradients(blocks, turned_q, turned_g, keys, values, turned_k, gathered):
    key_count, width = keys.shape
    heads = gathered.shape[1] // 3
    query_count = gathered.shape[2]
    chunk = (256, width)
    shapes = [chunk, (512, width), (512, width), chunk, chunk, (128, width), (128, width)]
    return pl.pallas_call(
        functools.partial(grad_kernel, width),
        out_shape=[array((width, heads * TILE // 2))] * 4 + [array(s) for s in shapes],
        in_specs=[SCALARS] + [SMALL] * 6,
        out_specs=[SMALL] * 11,
        scratch_shapes=[pltpu.VMEM((heads, query_count), F32)] * 2
        + [pltpu.VMEM((width, key_count), F32)] * 2
        + [pltpu.VMEM((key_count, width), F32)] * 2
        + [pltpu.VMEM((width, query_count * heads), F32)],
        compiler_params=vmem(24),
        name="grads",
    )(blocks, turned_q, turned_g, keys, values, turned_k, gathered)


def on_device(queries, keys, values, grad_out, query_blocks):
    queries, grad_out, keys, values, blocks = (
        pltpu.with_memory_space_constraint(x, pltpu.HBM) for x in (queries, grad_out, keys, values, query_blocks)
    )
    width = keys.shape[2]
    query_count = queries.shape[0]
    pb_size = lax.axis_size("pb")
    stats, turned_q, turned_g, own_k, own_v, turned_k = row_stats(blocks, queries, grad_out, keys, values)
    gathered = lax.all_gather(stats, "ka")

    dq0, dq1, dq2, dq3, own, near_p, near_m, far_p, far_m, half_p, half_m = gradients(
        blocks, turned_q, turned_g, own_k, own_v, turned_k, gathered
    )

    def along_z(x, by):
        return lax.ppermute(x, "pb", [(p, p // ZS * ZS + (p + by) % ZS) for p in range(pb_size)])

    def across_ka(x, by):
        return lax.ppermute(x, "ka", [(a, a ^ by) for a in range(4)])

    got_np = along_z(near_p, 1)
    got_nm = along_z(near_m, ZS - 1)
    got_hp = along_z(half_p, 2)
    got_hm = along_z(half_m, ZS - 2)

    got3 = across_ka(dq3, 1)
    got1 = across_ka(dq1, 1)
    far_p, far_m, for_other = pl.pallas_call(
        merge_kernel,
        out_shape=[array(far_p.shape), array(far_m.shape), array(dq2.shape)],
        in_specs=[SMALL] * 8,
        out_specs=[SMALL] * 3,
        compiler_params=vmem(8),
        name="merge",
    )(far_p, got_np, got_hp, far_m, got_nm, got_hm, dq2, got3)
    got_fp = along_z(far_p, 2)
    got_fm = along_z(far_m, ZS - 2)
    got2 = across_ka(for_other, 2)
    total = pl.pallas_call(
        sum_kernel,
        out_shape=array(own.shape),
        in_specs=[SMALL] * 5,
        out_specs=SMALL,
        compiler_params=vmem(8),
        name="add_parts",
    )(own, got_np, got_nm, got_fp, got_fm)
    lines = [list(range(z, pb_size, ZS)) for z in range(ZS)]
    parts = lax.all_to_all(total, "pb", 0, 0, axis_index_groups=lines, tiled=True)
    grad_keys, grad_values = pl.pallas_call(
        place_kernel,
        out_shape=[array((2, 64, width), BF16)] * 2,
        in_specs=[SMALL],
        out_specs=[SMALL] * 2,
        scratch_shapes=[pltpu.VMEM((2, 2, 8, 8, width), F32)],
        compiler_params=vmem(4),
        name="place_rows",
    )(parts)

    grad_queries = pl.pallas_call(
        query_kernel,
        out_shape=array((query_count // 4, queries.shape[1]), BF16),
        in_specs=[SMALL] * 3,
        out_specs=SMALL,
        compiler_params=vmem(8),
        name="finish_queries",
    )(dq0, got1, got2)
    return grad_queries, grad_keys, grad_values


def solution(mesh):
    placed = (P("pb", None), P(None, "ka", None), P(None, "ka", None), P("pb", None), P("pb"))
    return jax.shard_map(
        on_device,
        mesh=mesh,
        in_specs=placed,
        out_specs=(P(("pb", "ka"), None), P("ka", "pb", None), P("ka", "pb", None)),
        check_vma=False,
    )
```

```python
import functools
import math

import jax
import jax.numpy as jnp
from jax import lax
from jax.experimental import pallas as pl
from jax.experimental.pallas import tpu as pltpu
from jax.sharding import PartitionSpec as P

NEG = -1e30
HIDDEN = -2e30
TILE = 256
GROUP = 8
ZS = 8
YS = 4
F32 = jnp.float32
BF16 = jnp.bfloat16


def nt(a, b):
    return lax.dot_general(a, b, (((1,), (1,)), ((), ())), preferred_element_type=F32)


def nn(a, b):
    return jnp.dot(a, b, preferred_element_type=F32)


def own_head():
    return lax.axis_index("pb") // ZS


def own_z():
    return lax.axis_index("pb") % ZS


def for_tiles(blocks, work, before_slot=None):
    ka = lax.axis_index("ka")

    def step(u, n):
        slot = u // 4
        j = u % 4
        place = jnp.where(j < 2, 2 * ka + j, 2 * (7 - ka) + j - 2)
        block = blocks[slot]
        if before_slot is not None:
            pl.when(u == 4)(functools.partial(before_slot, 1))

        @pl.when(place < block)
        def _():
            work(slot, j, False, n)

        @pl.when(place == block)
        def _():
            work(slot, j, True, n)

        return n + jnp.where(place <= block, 1, 0)

    if before_slot is not None:
        before_slot(0)
    lax.fori_loop(0, 8, step, 0)


def rows_of(index, size):
    return pl.ds(pl.multiple_of(index * size, size), size)


def visible_mask():
    shape = (TILE, TILE)
    return lax.broadcasted_iota(jnp.int32, shape, 0) <= lax.broadcasted_iota(jnp.int32, shape, 1)


def stat_kernel(
    width, blocks, q_hbm, g_hbm, k_hbm, v_hbm,
    out_ref, qt_ref, gt_ref, k_ref, v_ref, kt_ref,
    q_ref, g_ref, m_scr, l_scr, d_scr, sems,
):
    def slot_rows(slot):
        return slice(slot * TILE, (slot + 1) * TILE)

    head = own_head()
    copies = [
        pltpu.make_async_copy(k_hbm.at[head], k_ref, sems.at[0]),
        pltpu.make_async_copy(v_hbm.at[head], v_ref, sems.at[1]),
    ]
    for slot in range(2):
        rows = slot_rows(slot)
        copies.append(pltpu.make_async_copy(q_hbm.at[rows], q_ref.at[rows], sems.at[2 + 2 * slot]))
        copies.append(pltpu.make_async_copy(g_hbm.at[rows], g_ref.at[rows], sems.at[3 + 2 * slot]))
    for copy in copies:
        copy.start()
    factor = width**-0.5 * math.log2(math.e)
    heads = out_ref.shape[0] // 2
    m_scr[...] = jnp.full(m_scr.shape, NEG, F32)
    l_scr[...] = jnp.zeros(l_scr.shape, F32)
    d_scr[...] = jnp.zeros(d_scr.shape, F32)

    def before_slot(slot):
        if slot == 0:
            for copy in copies[:2]:
                copy.wait()
            kt_ref[...] = k_ref[...].T
        for copy in copies[2 + 2 * slot : 4 + 2 * slot]:
            copy.wait()
        for h in range(heads):
            cols = slice(h * width, (h + 1) * width)
            at = (slot * heads + h) * TILE
            qt_ref[:, at : at + TILE] = q_ref[slot_rows(slot), cols].T
            gt_ref[:, at : at + TILE] = g_ref[slot_rows(slot), cols].T

    def work(slot, j, masked, n):
        keys = k_ref[rows_of(j, TILE), :]
        values = v_ref[rows_of(j, TILE), :]
        for h in range(heads):
            at = rows_of(slot * heads + h, TILE)
            scores = nn(keys, qt_ref[:, at]) * factor
            if masked:
                scores = jnp.where(visible_mask(), scores, HIDDEN)
            scores = scores.reshape(TILE // 8, 8, TILE)
            slopes = nn(values, gt_ref[:, at]).reshape(TILE // 8, 8, TILE)
            old = m_scr[h, slot]
            new = jnp.maximum(old, jnp.max(scores, axis=0))
            weights = jnp.exp2(scores - new[None])
            shrink = jnp.exp2(old - new)
            m_scr[h, slot] = new
            l_scr[h, slot] = l_scr[h, slot] * shrink + jnp.sum(weights, axis=0)
            d_scr[h, slot] = d_scr[h, slot] * shrink + jnp.sum(weights * slopes, axis=0)

    for_tiles(blocks, work, before_slot)
    for h in range(heads):
        for slot in range(2):
            cols = slot_rows(slot)
            m = m_scr[h, slot]
            top = jnp.max(m, axis=0, keepdims=True)
            shrink = jnp.exp2(m - top)
            total = jnp.sum(l_scr[h, slot] * shrink, axis=0, keepdims=True)
            dotted = jnp.sum(d_scr[h, slot] * shrink, axis=0, keepdims=True)
            out_ref[h : h + 1, cols] = top + jnp.log2(total)
            out_ref[heads + h : heads + h + 1, cols] = jnp.where(total > 0, dotted / total, 0.0)


def grad_kernel(
    width, blocks, qt_ref, gt_ref, k_ref, v_ref, stat_ref,
    stash, own, near_p, near_m, next_p, next_m, far_p, far_m, half_p, half_m,
    lse_scr, delta_scr, dk_scr, dv_scr, dk_rows, dv_rows,
):
    scale = width**-0.5
    factor = scale * math.log2(math.e)
    heads = lse_scr.shape[0]
    ka_size = stat_ref.shape[0]
    top = stat_ref[0, :heads, :]
    for a in range(1, ka_size):
        top = jnp.maximum(top, stat_ref[a, :heads, :])
    total = jnp.zeros(top.shape, F32)
    dotted = jnp.zeros(top.shape, F32)
    for a in range(ka_size):
        share = jnp.exp2(stat_ref[a, :heads, :] - top)
        total += share
        dotted += stat_ref[a, heads:, :] * share
    lse_scr[...] = top + jnp.log2(total)
    delta_scr[...] = dotted / total
    dk_scr[...] = jnp.zeros(dk_scr.shape, F32)
    dv_scr[...] = jnp.zeros(dv_scr.shape, F32)

    def work(slot, j, masked, n):
        keys = k_ref[rows_of(j, TILE), :]
        values = v_ref[rows_of(j, TILE), :]
        span = GROUP * TILE
        for first in range(0, heads, GROUP):
            at = pl.ds(pl.multiple_of((slot * heads + first) * TILE, TILE), span)
            qt = qt_ref[:, at]
            gt = gt_ref[:, at]
            lows, grads = [], []
            for i in range(GROUP):
                h = first + i
                part = slice(i * TILE, (i + 1) * TILE)
                lse = lse_scr[h : h + 1, rows_of(slot, TILE)]
                delta = delta_scr[h : h + 1, rows_of(slot, TILE)]
                probs = jnp.exp2(nn(keys, qt[:, part]) * factor - lse)
                if masked:
                    probs = jnp.where(visible_mask(), probs, 0.0)
                slopes = nn(values, gt[:, part])
                grads.append((probs * (slopes - delta) * scale).astype(BF16))
                lows.append(probs.astype(BF16))
            low = jnp.concatenate(lows, axis=1)
            grad = jnp.concatenate(grads, axis=1)
            stash[n, :, first * TILE : first * TILE + span] = grad
            dv_scr[:, rows_of(j, TILE)] += nt(gt, low)
            dk_scr[:, rows_of(j, TILE)] += nt(qt, grad)

    for_tiles(blocks, work)

    z = own_z()
    dk_rows[...] = dk_scr[...].T
    dv_rows[...] = dv_scr[...].T

    def put(out, at, rel, pieces):
        for g in pieces:
            row = lax.rem(z + rel, ZS) * 8 + g * 8 * ZS
            for acc in (dk_rows, dv_rows):
                for blk in range(2):
                    start = pl.multiple_of(row + blk * (dk_rows.shape[0] // 2), 8)
                    out[at : at + 8, :] = acc[pl.ds(start, 8), :]
                    at += 8

    every = range(8)
    put(own, 0, 0, every)
    put(near_p, 0, 3, every)
    put(near_m, 0, 5, every)
    put(next_p, 0, 1, every)
    put(next_m, 0, 7, every)
    put(far_p, 0, 2, every)
    put(far_m, 0, 6, every)
    put(half_p, 0, 4, range(4))
    put(half_m, 0, 4, range(4, 8))


def query_grad_kernel(blocks, kt_ref, stash, dq_near, dq_far, dq_core, dq_scr):
    dq_scr[...] = jnp.zeros(dq_scr.shape, F32)
    span = stash.shape[2]

    def work(slot, j, masked, n):
        del masked
        kt = kt_ref[:, rows_of(j, TILE)]
        dq_scr[:, rows_of(slot, span)] += nn(kt, stash[n])

    for_tiles(blocks, work)
    ka = lax.axis_index("ka")
    half = TILE // 2
    heads = span // TILE
    places = ((dq_near, 0), (dq_core, 0), (dq_far, 0), (dq_core, kt_ref.shape[0]))
    for rel, (out, at) in enumerate(places):
        share = jnp.bitwise_xor(ka, rel)
        slot, side = share // 2, share % 2
        for h in range(heads):
            start = pl.multiple_of((slot * heads + h) * TILE + side * half, half)
            out[at : at + kt_ref.shape[0], h * half : (h + 1) * half] = dq_scr[:, pl.ds(start, half)]


def merge_kernel(far_p, got_np, got_hp, far_m, got_nm, got_hm, out_p, out_m):
    half = got_hp.shape[0]
    out_p[:half] = far_p[:half] + got_np[:half] + got_hp[...]
    out_p[half:] = far_p[half:] + got_np[half:]
    out_m[:half] = far_m[:half] + got_nm[:half]
    out_m[half:] = far_m[half:] + got_nm[half:] + got_hm[...]


def sum_kernel(own, next_p, next_m, far_p, far_m, out):
    out[...] = (own[...] + next_p[...] + next_m[...]) + (far_p[...] + far_m[...])


def place_kernel(parts, dk_ref, dv_ref, scr):
    for head in range(parts.shape[0] // 32):
        for kv in range(2):
            for blk in range(2):
                at = head * 32 + (kv * 2 + blk) * 8
                scr[kv, blk, :, head : head + 1, :] = parts[at : at + 8, :].reshape(8, 1, parts.shape[1])
    for kv, out in enumerate((dk_ref, dv_ref)):
        for blk in range(2):
            out[blk] = scr[kv, blk].reshape(64, out.shape[2]).astype(BF16)


def add_kernel(a_ref, b_ref, out_ref):
    out_ref[...] = a_ref[...] + b_ref[a_ref.shape[0] :]


def query_kernel(a_ref, b_ref, c_ref, out_ref):
    rows, width = out_ref.shape[0], a_ref.shape[0]
    for h in range(out_ref.shape[1] // width):
        part = slice(h * rows, (h + 1) * rows)
        total = a_ref[:, part] + b_ref[:width, part] + c_ref[:, part]
        out_ref[:, h * width : (h + 1) * width] = total.T.astype(BF16)


def array(shape, dtype=F32):
    return jax.ShapeDtypeStruct(shape, dtype)


SMALL = pl.BlockSpec(memory_space=pltpu.VMEM)
SCALARS = pl.BlockSpec(memory_space=pltpu.SMEM)
LARGE = pl.BlockSpec(memory_space=pltpu.HBM)


def cost(us):
    return pl.CostEstimate(flops=int(us * 1.15e9), bytes_accessed=0, transcendentals=0)


def vmem(mib):
    return pltpu.CompilerParams(vmem_limit_bytes=int(mib * 2**20))


def row_stats(blocks, queries, grad_out, keys, values):
    _, key_count, width = keys.shape
    query_count = queries.shape[0]
    heads = queries.shape[1] // width
    turned = array((width, query_count * heads), BF16)
    own = array((key_count, width), BF16)
    return pl.pallas_call(
        functools.partial(stat_kernel, width),
        out_shape=[array((2 * heads, query_count)), turned, turned, own, own, array((width, key_count), BF16)],
        in_specs=[SCALARS] + [LARGE] * 4,
        out_specs=[SMALL] * 6,
        scratch_shapes=[pltpu.VMEM(queries.shape, BF16)] * 2
        + [pltpu.VMEM((heads, 2, 8, TILE), F32)] * 3
        + [pltpu.SemaphoreType.DMA((6,))],
        compiler_params=vmem(24),
        name="row_stats",
    )(blocks, queries, grad_out, keys, values)


def key_gradients(blocks, turned_q, turned_g, keys, values, gathered):
    key_count, width = keys.shape
    heads = gathered.shape[1] // 2
    query_count = gathered.shape[2]
    chunk = (256, width)
    shapes = [chunk] * 7 + [(128, width)] * 2
    return pl.pallas_call(
        functools.partial(grad_kernel, width),
        out_shape=[array((5, TILE, heads * TILE), BF16)] + [array(s) for s in shapes],
        in_specs=[SCALARS] + [SMALL] * 5,
        out_specs=[SMALL] * 10,
        scratch_shapes=[pltpu.VMEM((heads, query_count), F32)] * 2
        + [pltpu.VMEM((width, key_count), F32)] * 2
        + [pltpu.VMEM((key_count, width), F32)] * 2,
        compiler_params=vmem(24),
        name="key_grads",
    )(blocks, turned_q, turned_g, keys, values, gathered)


def query_gradients(blocks, turned_k, stash):
    width = turned_k.shape[0]
    span = stash.shape[2]
    return pl.pallas_call(
        query_grad_kernel,
        out_shape=[array((width, span // 2))] * 2 + [array((2 * width, span // 2))],
        in_specs=[SCALARS, SMALL, SMALL],
        out_specs=[SMALL] * 3,
        scratch_shapes=[pltpu.VMEM((width, 2 * span), F32)],
        compiler_params=vmem(16),
        cost_estimate=cost(2.5),
        name="query_grads",
    )(blocks, turned_k, stash)


def on_device(queries, keys, values, grad_out, query_blocks):
    queries, grad_out, keys, values, blocks = (
        pltpu.with_memory_space_constraint(x, pltpu.HBM) for x in (queries, grad_out, keys, values, query_blocks)
    )
    width = keys.shape[2]
    query_count = queries.shape[0]
    pb_size = lax.axis_size("pb")
    stats, turned_q, turned_g, own_k, own_v, turned_k = row_stats(blocks, queries, grad_out, keys, values)
    gathered = lax.all_gather(stats, "ka")

    stash, own, near_p, near_m, next_p, next_m, far_p, far_m, half_p, half_m = key_gradients(
        blocks, turned_q, turned_g, own_k, own_v, gathered
    )

    def along_z(x, by):
        return lax.ppermute(x, "pb", [(p, p // ZS * ZS + (p + by) % ZS) for p in range(pb_size)])

    def across_ka(x, by):
        return lax.ppermute(x, "ka", [(a, a ^ by) for a in range(4)])

    got_np = along_z(near_p, 1)
    got_nm = along_z(near_m, ZS - 1)
    got_hp = along_z(half_p, 2)
    next_p = along_z(next_p, 1)
    next_m = along_z(next_m, ZS - 1)
    got_hm = along_z(half_m, ZS - 2)

    dq_near, dq_far, dq_core = query_gradients(blocks, turned_k, stash)
    got_core = across_ka(dq_core, 1)
    for_other = pl.pallas_call(
        add_kernel,
        out_shape=array(dq_far.shape),
        in_specs=[SMALL] * 2,
        out_specs=SMALL,
        compiler_params=vmem(4),
        name="add_queries",
    )(dq_far, got_core)
    got_far = across_ka(for_other, 2)
    far_p, far_m = pl.pallas_call(
        merge_kernel,
        out_shape=[array(far_p.shape), array(far_m.shape)],
        in_specs=[SMALL] * 6,
        out_specs=[SMALL] * 2,
        compiler_params=vmem(8),
        cost_estimate=cost(10),
        name="merge",
    )(far_p, got_np, got_hp, far_m, got_nm, got_hm)
    got_fp = along_z(far_p, 2)
    got_fm = along_z(far_m, ZS - 2)
    total = pl.pallas_call(
        sum_kernel,
        out_shape=array(own.shape),
        in_specs=[SMALL] * 5,
        out_specs=SMALL,
        compiler_params=vmem(8),
        name="add_parts",
    )(own, next_p, next_m, got_fp, got_fm)
    lines = [list(range(z, pb_size, ZS)) for z in range(ZS)]
    parts = lax.all_to_all(total, "pb", 0, 0, axis_index_groups=lines, tiled=True)
    grad_keys, grad_values = pl.pallas_call(
        place_kernel,
        out_shape=[array((2, 64, width), BF16)] * 2,
        in_specs=[SMALL],
        out_specs=[SMALL] * 2,
        scratch_shapes=[pltpu.VMEM((2, 2, 8, 8, width), F32)],
        compiler_params=vmem(4),
        cost_estimate=cost(3),
        name="place_rows",
    )(parts)

    grad_queries = pl.pallas_call(
        query_kernel,
        out_shape=array((query_count // 4, queries.shape[1]), BF16),
        in_specs=[SMALL] * 3,
        out_specs=SMALL,
        compiler_params=vmem(8),
        name="finish_queries",
    )(dq_near, got_core, got_far)
    return grad_queries, grad_keys, grad_values


def solution(mesh):
    placed = (P("pb", None), P(None, "ka", None), P(None, "ka", None), P("pb", None), P("pb"))
    return jax.shard_map(
        on_device,
        mesh=mesh,
        in_specs=placed,
        out_specs=(P(("pb", "ka"), None), P("ka", "pb", None), P("ka", "pb", None)),
        check_vma=False,
    )
```

```python
import functools
import math

import jax
import jax.numpy as jnp
from jax import lax
from jax.experimental import pallas as pl
from jax.experimental.pallas import tpu as pltpu
from jax.sharding import PartitionSpec as P

NEG = -1e30
HIDDEN = -2e30
TILE = 256
GROUP = 4
ZS = 8
YS = 4
F32 = jnp.float32
BF16 = jnp.bfloat16


def nt(a, b):
    return lax.dot_general(a, b, (((1,), (1,)), ((), ())), preferred_element_type=F32)


def nn(a, b):
    return jnp.dot(a, b, preferred_element_type=F32)


def own_head():
    return lax.axis_index("pb") // ZS


def own_z():
    return lax.axis_index("pb") % ZS


def for_tiles(blocks, work, before_slot=None):
    ka = lax.axis_index("ka")

    def step(u, n):
        slot = u // 4
        j = u % 4
        place = jnp.where(j < 2, 2 * ka + j, 2 * (7 - ka) + j - 2)
        block = blocks[slot]
        if before_slot is not None:
            pl.when(u == 4)(functools.partial(before_slot, 1))

        @pl.when(place < block)
        def _():
            work(slot, j, False, n)

        @pl.when(place == block)
        def _():
            work(slot, j, True, n)

        return n + jnp.where(place <= block, 1, 0)

    if before_slot is not None:
        before_slot(0)
    lax.fori_loop(0, 8, step, 0)


def rows_of(index, size):
    return pl.ds(pl.multiple_of(index * size, size), size)


def visible_mask():
    shape = (TILE, TILE)
    return lax.broadcasted_iota(jnp.int32, shape, 0) <= lax.broadcasted_iota(jnp.int32, shape, 1)


def slot_rows(slot):
    return slice(slot * TILE, (slot + 1) * TILE)


def copies_in(q_hbm, g_hbm, k_hbm, v_hbm, q_ref, g_ref, k_ref, v_ref, sems):
    head = own_head()
    pairs = [(k_hbm.at[head], k_ref), (v_hbm.at[head], v_ref)]
    for slot in range(2):
        rows = slot_rows(slot)
        pairs += [(q_hbm.at[rows], q_ref.at[rows]), (g_hbm.at[rows], g_ref.at[rows])]
    return [pltpu.make_async_copy(src, dst, sems.at[i]) for i, (src, dst) in enumerate(pairs)]


def stat_kernel(
    width, blocks, q_hbm, g_hbm, k_hbm, v_hbm, out_ref,
    q_ref, g_ref, k_ref, v_ref, m_scr, l_scr, d_scr, sems,
):
    copies = copies_in(q_hbm, g_hbm, k_hbm, v_hbm, q_ref, g_ref, k_ref, v_ref, sems)
    for copy in copies:
        copy.start()
    factor = width**-0.5 * math.log2(math.e)
    heads = out_ref.shape[0] // 2
    m_scr[...] = jnp.full(m_scr.shape, NEG, F32)
    l_scr[...] = jnp.zeros(l_scr.shape, F32)
    d_scr[...] = jnp.zeros(d_scr.shape, F32)

    def before_slot(slot):
        for copy in copies[:2] * (slot == 0) + copies[2 + 2 * slot : 4 + 2 * slot]:
            copy.wait()

    def work(slot, j, masked, n):
        keys = k_ref[rows_of(j, TILE), :]
        values = v_ref[rows_of(j, TILE), :]
        for h in range(heads):
            cols = slice(h * width, (h + 1) * width)
            scores = nt(keys, q_ref[rows_of(slot, TILE), cols]) * factor
            if masked:
                scores = jnp.where(visible_mask(), scores, HIDDEN)
            scores = scores.reshape(TILE // 8, 8, TILE)
            slopes = nt(values, g_ref[rows_of(slot, TILE), cols]).reshape(TILE // 8, 8, TILE)
            old = m_scr[h, slot]
            new = jnp.maximum(old, jnp.max(scores, axis=0))
            weights = jnp.exp2(scores - new[None])
            shrink = jnp.exp2(old - new)
            m_scr[h, slot] = new
            l_scr[h, slot] = l_scr[h, slot] * shrink + jnp.sum(weights, axis=0)
            d_scr[h, slot] = d_scr[h, slot] * shrink + jnp.sum(weights * slopes, axis=0)

    for_tiles(blocks, work, before_slot)
    for h in range(heads):
        for slot in range(2):
            cols = slot_rows(slot)
            m = m_scr[h, slot]
            top = jnp.max(m, axis=0, keepdims=True)
            shrink = jnp.exp2(m - top)
            total = jnp.sum(l_scr[h, slot] * shrink, axis=0, keepdims=True)
            dotted = jnp.sum(d_scr[h, slot] * shrink, axis=0, keepdims=True)
            out_ref[h : h + 1, cols] = top + jnp.log2(total)
            out_ref[heads + h : heads + h + 1, cols] = jnp.where(total > 0, dotted / total, 0.0)


def turn_kernel(
    q_hbm, g_hbm, k_hbm, v_hbm, qt_ref, gt_ref, k_ref, v_ref, kt_ref, q_ref, g_ref, sems
):
    copies = copies_in(q_hbm, g_hbm, k_hbm, v_hbm, q_ref, g_ref, k_ref, v_ref, sems)
    width = k_ref.shape[1]
    heads = q_ref.shape[1] // width
    for copy in copies:
        copy.start()
    for copy in copies[:2]:
        copy.wait()
    kt_ref[...] = k_ref[...].T
    for slot in range(2):
        for copy in copies[2 + 2 * slot : 4 + 2 * slot]:
            copy.wait()
        for h in range(heads):
            cols = slice(h * width, (h + 1) * width)
            at = (slot * heads + h) * TILE
            qt_ref[:, at : at + TILE] = q_ref[slot_rows(slot), cols].T
            gt_ref[:, at : at + TILE] = g_ref[slot_rows(slot), cols].T


def grad_kernel(
    width, blocks, qt_ref, gt_ref, k_ref, v_ref, *refs,
):
    grad_body(width, blocks, qt_ref, gt_ref, k_ref, v_ref, refs[:4], *refs[4:])


def grad_body(
    width, blocks, qt_ref, gt_ref, k_ref, v_ref, stats,
    stash, own, near_p, near_m, next_p, next_m, far_p, far_m, half_p, half_m,
    lse_scr, delta_scr, dk_scr, dv_scr, dk_rows, dv_rows,
):
    scale = width**-0.5
    factor = scale * math.log2(math.e)
    heads = lse_scr.shape[0]
    top = stats[0][:heads]
    for stat in stats[1:]:
        top = jnp.maximum(top, stat[:heads])
    total = jnp.zeros(top.shape, F32)
    dotted = jnp.zeros(top.shape, F32)
    for stat in stats:
        share = jnp.exp2(stat[:heads] - top)
        total += share
        dotted += stat[heads:] * share
    lse_scr[...] = top + jnp.log2(total)
    delta_scr[...] = dotted / total
    dk_scr[...] = jnp.zeros(dk_scr.shape, F32)
    dv_scr[...] = jnp.zeros(dv_scr.shape, F32)

    def work(slot, j, masked, n):
        keys = k_ref[rows_of(j, TILE), :]
        values = v_ref[rows_of(j, TILE), :]
        span = GROUP * TILE
        value_sum = dv_scr[:, rows_of(j, TILE)]
        key_sum = dk_scr[:, rows_of(j, TILE)]
        for first in range(0, heads, GROUP):
            at = pl.ds(pl.multiple_of((slot * heads + first) * TILE, TILE), span)
            qt = qt_ref[:, at]
            gt = gt_ref[:, at]
            lows, grads = [], []
            for i in range(GROUP):
                h = first + i
                part = slice(i * TILE, (i + 1) * TILE)
                lse = lse_scr[h : h + 1, rows_of(slot, TILE)]
                delta = delta_scr[h : h + 1, rows_of(slot, TILE)]
                probs = jnp.exp2(nn(keys, qt[:, part]) * factor - lse)
                if masked:
                    probs = jnp.where(visible_mask(), probs, 0.0)
                slopes = nn(values, gt[:, part])
                grads.append((probs * (slopes - delta) * scale).astype(BF16))
                lows.append(probs.astype(BF16))
            low = jnp.concatenate(lows, axis=1)
            grad = jnp.concatenate(grads, axis=1)
            stash[n, :, first * TILE : first * TILE + span] = grad
            value_sum = value_sum + nt(gt, low)
            key_sum = key_sum + nt(qt, grad)
        dv_scr[:, rows_of(j, TILE)] = value_sum
        dk_scr[:, rows_of(j, TILE)] = key_sum

    for_tiles(blocks, work)

    z = own_z()
    dk_rows[...] = dk_scr[...].T
    dv_rows[...] = dv_scr[...].T

    def put(out, at, rel, pieces):
        for g in pieces:
            row = lax.rem(z + rel, ZS) * 8 + g * 8 * ZS
            for acc in (dk_rows, dv_rows):
                for blk in range(2):
                    start = pl.multiple_of(row + blk * (dk_rows.shape[0] // 2), 8)
                    out[at : at + 8, :] = acc[pl.ds(start, 8), :]
                    at += 8

    every = range(8)
    put(own, 0, 0, every)
    put(near_p, 0, 3, every)
    put(near_m, 0, 5, every)
    put(next_p, 0, 1, every)
    put(next_m, 0, 7, every)
    put(far_p, 0, 2, every)
    put(far_m, 0, 6, every)
    put(half_p, 0, 4, range(4))
    put(half_m, 0, 4, range(4, 8))


def query_grad_kernel(blocks, kt_ref, stash, dq_near, dq_far, dq_core, dq_scr):
    dq_scr[...] = jnp.zeros(dq_scr.shape, F32)
    span = stash.shape[2]

    def work(slot, j, masked, n):
        del masked
        kt = kt_ref[:, rows_of(j, TILE)]
        dq_scr[:, rows_of(slot, span)] += nn(kt, stash[n])

    for_tiles(blocks, work)
    ka = lax.axis_index("ka")
    half = TILE // 2
    heads = span // TILE
    places = ((dq_near, 0), (dq_core, 0), (dq_far, 0), (dq_core, kt_ref.shape[0]))
    for rel, (out, at) in enumerate(places):
        share = jnp.bitwise_xor(ka, rel)
        slot, side = share // 2, share % 2
        for h in range(heads):
            start = pl.multiple_of((slot * heads + h) * TILE + side * half, half)
            out[at : at + kt_ref.shape[0], h * half : (h + 1) * half] = dq_scr[:, pl.ds(start, half)]


def merge_kernel(far_p, got_np, got_hp, far_m, got_nm, got_hm, out_p, out_m):
    half = got_hp.shape[0]
    out_p[:half] = far_p[:half] + got_np[:half] + got_hp[...]
    out_p[half:] = far_p[half:] + got_np[half:]
    out_m[:half] = far_m[:half] + got_nm[:half]
    out_m[half:] = far_m[half:] + got_nm[half:] + got_hm[...]


def sum_kernel(own, next_p, next_m, far_p, far_m, *outs):
    xh, y = own_head() // YS, own_head() % YS
    size = outs[0].shape[1]
    for rel, out in enumerate(outs):
        for i, x in enumerate((xh, 1 - xh)):
            rows = rows_of(x * YS + lax.rem(y + rel, YS), size)
            out[i] = (own[rows, :] + next_p[rows, :] + next_m[rows, :]) + (far_p[rows, :] + far_m[rows, :])


def cross_kernel(own, from1, from2, from3, out):
    for rel, part in enumerate((own, from1, from2, from3)):
        out[rel] = part[1]


def place_kernel(own, from1, from2, from3, crossed, after, dk_ref, dv_ref, scr):
    del after
    xh, y = own_head() // YS, own_head() % YS
    for rel, near in enumerate((own, from1, from2, from3)):
        from_y = lax.rem(y + YS - rel, YS)
        for part, from_x in ((near[0], xh), (crossed[rel], 1 - xh)):
            head = from_x * YS + from_y
            for kv in range(2):
                for blk in range(2):
                    at = (kv * 2 + blk) * 8
                    scr[kv, blk, :, pl.ds(head, 1), :] = part[at : at + 8, :].reshape(8, 1, part.shape[1])
    for kv, out in enumerate((dk_ref, dv_ref)):
        for blk in range(2):
            out[blk] = scr[kv, blk].reshape(64, out.shape[2]).astype(BF16)


def add_kernel(a_ref, b_ref, out_ref):
    out_ref[...] = a_ref[...] + b_ref[a_ref.shape[0] :]


def query_kernel(a_ref, b_ref, c_ref, out_ref, token_ref):
    token_ref[...] = jnp.zeros(token_ref.shape, F32)
    rows, width = out_ref.shape[0], a_ref.shape[0]
    for h in range(out_ref.shape[1] // width):
        part = slice(h * rows, (h + 1) * rows)
        total = a_ref[:, part] + b_ref[:width, part] + c_ref[:, part]
        out_ref[:, h * width : (h + 1) * width] = total.T.astype(BF16)


def array(shape, dtype=F32):
    return jax.ShapeDtypeStruct(shape, dtype)


SMALL = pl.BlockSpec(memory_space=pltpu.VMEM)
SCALARS = pl.BlockSpec(memory_space=pltpu.SMEM)
LARGE = pl.BlockSpec(memory_space=pltpu.HBM)


def cost(us):
    return pl.CostEstimate(flops=int(us * 1.15e9), bytes_accessed=0, transcendentals=0)


def vmem(mib):
    return pltpu.CompilerParams(vmem_limit_bytes=int(mib * 2**20))


def row_stats(blocks, queries, grad_out, keys, values):
    _, key_count, width = keys.shape
    query_count = queries.shape[0]
    heads = queries.shape[1] // width
    return pl.pallas_call(
        functools.partial(stat_kernel, width),
        out_shape=array((2 * heads, query_count)),
        in_specs=[SCALARS] + [LARGE] * 4,
        out_specs=SMALL,
        scratch_shapes=[pltpu.VMEM(queries.shape, BF16)] * 2
        + [pltpu.VMEM((key_count, width), BF16)] * 2
        + [pltpu.VMEM((heads, 2, 8, TILE), F32)] * 3
        + [pltpu.SemaphoreType.DMA((6,))],
        compiler_params=vmem(24),
        name="row_stats",
    )(blocks, queries, grad_out, keys, values)


def turned_inputs(queries, grad_out, keys, values):
    _, key_count, width = keys.shape
    turned = array((width, queries.size // width), BF16)
    own = array((key_count, width), BF16)
    return pl.pallas_call(
        turn_kernel,
        out_shape=[turned, turned, own, own, array((width, key_count), BF16)],
        in_specs=[LARGE] * 4,
        out_specs=[SMALL] * 5,
        scratch_shapes=[pltpu.VMEM(queries.shape, BF16)] * 2 + [pltpu.SemaphoreType.DMA((6,))],
        compiler_params=vmem(16),
        cost_estimate=cost(3),
        name="turn_inputs",
    )(queries, grad_out, keys, values)


def key_gradients(blocks, turned_q, turned_g, keys, values, stats):
    key_count, width = keys.shape
    heads = stats[0].shape[0] // 2
    query_count = stats[0].shape[1]
    chunk = (256, width)
    shapes = [chunk] * 7 + [(128, width)] * 2
    return pl.pallas_call(
        functools.partial(grad_kernel, width),
        out_shape=[array((5, TILE, heads * TILE), BF16)] + [array(s) for s in shapes],
        in_specs=[SCALARS] + [SMALL] * 8,
        out_specs=[SMALL] * 10,
        scratch_shapes=[pltpu.VMEM((heads, query_count), F32)] * 2
        + [pltpu.VMEM((width, key_count), F32)] * 2
        + [pltpu.VMEM((key_count, width), F32)] * 2,
        compiler_params=vmem(24),
        name="key_grads",
    )(blocks, turned_q, turned_g, keys, values, *stats)


def query_gradients(blocks, turned_k, stash):
    width = turned_k.shape[0]
    span = stash.shape[2]
    return pl.pallas_call(
        query_grad_kernel,
        out_shape=[array((width, span // 2))] * 2 + [array((2 * width, span // 2))],
        in_specs=[SCALARS] + [SMALL] * 2,
        out_specs=[SMALL] * 3,
        scratch_shapes=[pltpu.VMEM((width, 2 * span), F32)],
        compiler_params=vmem(16),
        cost_estimate=cost(2.5),
        name="query_grads",
    )(blocks, turned_k, stash)


def on_device(queries, keys, values, grad_out, query_blocks):
    queries, grad_out, keys, values, blocks = (
        pltpu.with_memory_space_constraint(x, pltpu.HBM) for x in (queries, grad_out, keys, values, query_blocks)
    )
    width = keys.shape[2]
    query_count = queries.shape[0]
    pb_size = lax.axis_size("pb")

    def across_ka(x, by):
        return lax.ppermute(x, "ka", [(a, a ^ by) for a in range(4)])

    own_stats = row_stats(blocks, queries, grad_out, keys, values)
    stats = [own_stats] + [across_ka(own_stats, by) for by in (2, 3, 1)]
    turned_q, turned_g, own_k, own_v, turned_k = turned_inputs(queries, grad_out, keys, values)
    stash, own, near_p, near_m, next_p, next_m, far_p, far_m, half_p, half_m = key_gradients(
        blocks, turned_q, turned_g, own_k, own_v, stats
    )

    def along_y(x, by):
        return lax.ppermute(
            x, "pb", [(p, (p // (ZS * YS) * YS + (p // ZS + by) % YS) * ZS + p % ZS) for p in range(pb_size)]
        )

    def along_z(x, by):
        return lax.ppermute(x, "pb", [(p, p // ZS * ZS + (p + by) % ZS) for p in range(pb_size)])

    got_np = along_z(near_p, 1)
    got_nm = along_z(near_m, ZS - 1)
    got_hp = along_z(half_p, 2)
    got_hm = along_z(half_m, ZS - 2)

    dq_near, dq_far, dq_core = query_gradients(blocks, turned_k, stash)
    next_p = along_z(next_p, 1)
    next_m = along_z(next_m, ZS - 1)
    got_core = across_ka(dq_core, 1)
    for_other = pl.pallas_call(
        add_kernel,
        out_shape=array(dq_far.shape),
        in_specs=[SMALL] * 2,
        out_specs=SMALL,
        compiler_params=vmem(4),
        name="add_queries",
    )(dq_far, got_core)
    got_far = across_ka(for_other, 2)
    far_p, far_m = pl.pallas_call(
        merge_kernel,
        out_shape=[array(far_p.shape), array(far_m.shape)],
        in_specs=[SMALL] * 6,
        out_specs=[SMALL] * 2,
        compiler_params=vmem(8),
        cost_estimate=cost(10),
        name="merge",
    )(far_p, got_np, got_hp, far_m, got_nm, got_hm)
    got_fp = along_z(far_p, 2)
    got_fm = along_z(far_m, ZS - 2)
    parts = pl.pallas_call(
        sum_kernel,
        out_shape=[array((2, 32, width))] * YS,
        in_specs=[SMALL] * 5,
        out_specs=[SMALL] * YS,
        compiler_params=vmem(8),
        name="add_parts",
    )(own, next_p, next_m, got_fp, got_fm)
    parts = [parts[0]] + [along_y(parts[k], k) for k in range(1, YS)]
    crossed = pl.pallas_call(
        cross_kernel,
        out_shape=array((YS, 32, width)),
        in_specs=[SMALL] * YS,
        out_specs=SMALL,
        compiler_params=vmem(4),
        cost_estimate=cost(3),
        name="cross_parts",
    )(*parts)
    crossed = lax.ppermute(crossed, "pb", [(p, (p + pb_size // 2) % pb_size) for p in range(pb_size)])
    grad_queries, token = pl.pallas_call(
        query_kernel,
        out_shape=[array((query_count // 4, queries.shape[1]), BF16), array((8, 128))],
        in_specs=[SMALL] * 3,
        out_specs=[SMALL] * 2,
        compiler_params=vmem(8),
        name="finish_queries",
    )(dq_near, got_core, got_far)
    grad_keys, grad_values = pl.pallas_call(
        place_kernel,
        out_shape=[array((2, 64, width), BF16)] * 2,
        in_specs=[SMALL] * (YS + 1) + [pl.BlockSpec(memory_space=pl.ANY)],
        out_specs=[SMALL] * 2,
        scratch_shapes=[pltpu.VMEM((2, 2, 8, 8, width), F32)],
        compiler_params=vmem(4),
        cost_estimate=cost(3),
        name="place_rows",
    )(*parts, crossed, token)

    return grad_queries, grad_keys, grad_values


def solution(mesh):
    placed = (P("pb", None), P(None, "ka", None), P(None, "ka", None), P("pb", None), P("pb"))
    return jax.shard_map(
        on_device,
        mesh=mesh,
        in_specs=placed,
        out_specs=(P(("pb", "ka"), None), P("ka", "pb", None), P("ka", "pb", None)),
        check_vma=False,
    )
```

```python
import functools
import math

import jax
import jax.numpy as jnp
from jax import lax
from jax.experimental import pallas as pl
from jax.experimental.pallas import tpu as pltpu
from jax.sharding import PartitionSpec as P

NEG = -1e30
HIDDEN = -2e30
TILE = 256
GROUP = 4
ZS = 8
YS = 4
F32 = jnp.float32
BF16 = jnp.bfloat16


def nt(a, b):
    return lax.dot_general(a, b, (((1,), (1,)), ((), ())), preferred_element_type=F32)


def nn(a, b):
    return jnp.dot(a, b, preferred_element_type=F32)


def own_head():
    return lax.axis_index("pb") // ZS


def own_z():
    return lax.axis_index("pb") % ZS


def for_tiles(blocks, work, before_slot=None):
    ka = lax.axis_index("ka")

    def step(u, n):
        slot = u // 4
        j = u % 4
        place = jnp.where(j < 2, 2 * ka + j, 2 * (7 - ka) + j - 2)
        block = blocks[slot]
        if before_slot is not None:
            pl.when(u == 4)(functools.partial(before_slot, 1))

        @pl.when(place < block)
        def _():
            work(slot, j, False, n)

        @pl.when(place == block)
        def _():
            work(slot, j, True, n)

        return n + jnp.where(place <= block, 1, 0)

    if before_slot is not None:
        before_slot(0)
    lax.fori_loop(0, 8, step, 0)


def rows_of(index, size):
    return pl.ds(pl.multiple_of(index * size, size), size)


def visible_mask():
    shape = (TILE, TILE)
    return lax.broadcasted_iota(jnp.int32, shape, 0) <= lax.broadcasted_iota(jnp.int32, shape, 1)


def slot_rows(slot):
    return slice(slot * TILE, (slot + 1) * TILE)


def copies_in(q_hbm, g_hbm, k_hbm, v_hbm, q_ref, g_ref, k_ref, v_ref, sems):
    head = own_head()
    pairs = [(k_hbm.at[head], k_ref), (v_hbm.at[head], v_ref)]
    for slot in range(2):
        rows = slot_rows(slot)
        pairs += [(q_hbm.at[rows], q_ref.at[rows]), (g_hbm.at[rows], g_ref.at[rows])]
    return [pltpu.make_async_copy(src, dst, sems.at[i]) for i, (src, dst) in enumerate(pairs)]


def stat_kernel(
    width, blocks, q_hbm, g_hbm, k_hbm, v_hbm, out_ref,
    q_ref, g_ref, k_ref, v_ref, m_scr, l_scr, d_scr, sems,
):
    copies = copies_in(q_hbm, g_hbm, k_hbm, v_hbm, q_ref, g_ref, k_ref, v_ref, sems)
    for copy in copies:
        copy.start()
    factor = width**-0.5 * math.log2(math.e)
    heads = out_ref.shape[0] // 2
    m_scr[...] = jnp.full(m_scr.shape, NEG, F32)
    l_scr[...] = jnp.zeros(l_scr.shape, F32)
    d_scr[...] = jnp.zeros(d_scr.shape, F32)

    def before_slot(slot):
        for copy in copies[:2] * (slot == 0) + copies[2 + 2 * slot : 4 + 2 * slot]:
            copy.wait()

    def work(slot, j, masked, n):
        keys = k_ref[rows_of(j, TILE), :]
        values = v_ref[rows_of(j, TILE), :]
        for h in range(heads):
            cols = slice(h * width, (h + 1) * width)
            scores = nt(keys, q_ref[rows_of(slot, TILE), cols]) * factor
            if masked:
                scores = jnp.where(visible_mask(), scores, HIDDEN)
            scores = scores.reshape(TILE // 8, 8, TILE)
            slopes = nt(values, g_ref[rows_of(slot, TILE), cols]).reshape(TILE // 8, 8, TILE)
            old = m_scr[h, slot]
            new = jnp.maximum(old, jnp.max(scores, axis=0))
            weights = jnp.exp2(scores - new[None])
            shrink = jnp.exp2(old - new)
            m_scr[h, slot] = new
            l_scr[h, slot] = l_scr[h, slot] * shrink + jnp.sum(weights, axis=0)
            d_scr[h, slot] = d_scr[h, slot] * shrink + jnp.sum(weights * slopes, axis=0)

    for_tiles(blocks, work, before_slot)
    for h in range(heads):
        for slot in range(2):
            cols = slot_rows(slot)
            m = m_scr[h, slot]
            top = jnp.max(m, axis=0, keepdims=True)
            shrink = jnp.exp2(m - top)
            total = jnp.sum(l_scr[h, slot] * shrink, axis=0, keepdims=True)
            dotted = jnp.sum(d_scr[h, slot] * shrink, axis=0, keepdims=True)
            out_ref[h : h + 1, cols] = top + jnp.log2(total)
            out_ref[heads + h : heads + h + 1, cols] = jnp.where(total > 0, dotted / total, 0.0)


def turn_kernel(
    q_hbm, g_hbm, k_hbm, v_hbm, qt_ref, gt_ref, k_ref, v_ref, kt_ref, q_ref, g_ref, sems
):
    copies = copies_in(q_hbm, g_hbm, k_hbm, v_hbm, q_ref, g_ref, k_ref, v_ref, sems)
    width = k_ref.shape[1]
    heads = q_ref.shape[1] // width
    for copy in copies:
        copy.start()
    for copy in copies[:2]:
        copy.wait()
    kt_ref[...] = k_ref[...].T
    for slot in range(2):
        for copy in copies[2 + 2 * slot : 4 + 2 * slot]:
            copy.wait()
        for h in range(heads):
            cols = slice(h * width, (h + 1) * width)
            at = (slot * heads + h) * TILE
            qt_ref[:, at : at + TILE] = q_ref[slot_rows(slot), cols].T
            gt_ref[:, at : at + TILE] = g_ref[slot_rows(slot), cols].T


def grad_kernel(
    width, blocks, qt_ref, gt_ref, k_ref, v_ref, *refs,
):
    grad_body(width, blocks, qt_ref, gt_ref, k_ref, v_ref, refs[:4], *refs[4:])


def grad_body(
    width, blocks, qt_ref, gt_ref, k_ref, v_ref, stats,
    stash, own, near_p, near_m, next_p, next_m, far_p, far_m, across,
    lse_scr, delta_scr, dk_scr, dv_scr, dk_rows, dv_rows,
):
    scale = width**-0.5
    factor = scale * math.log2(math.e)
    heads = lse_scr.shape[0]
    top = stats[0][:heads]
    for stat in stats[1:]:
        top = jnp.maximum(top, stat[:heads])
    total = jnp.zeros(top.shape, F32)
    dotted = jnp.zeros(top.shape, F32)
    for stat in stats:
        share = jnp.exp2(stat[:heads] - top)
        total += share
        dotted += stat[heads:] * share
    lse_scr[...] = top + jnp.log2(total)
    delta_scr[...] = dotted / total
    dk_scr[...] = jnp.zeros(dk_scr.shape, F32)
    dv_scr[...] = jnp.zeros(dv_scr.shape, F32)

    def work(slot, j, masked, n):
        keys = k_ref[rows_of(j, TILE), :]
        values = v_ref[rows_of(j, TILE), :]
        span = GROUP * TILE
        value_sum = dv_scr[:, rows_of(j, TILE)]
        key_sum = dk_scr[:, rows_of(j, TILE)]
        for first in range(0, heads, GROUP):
            at = pl.ds(pl.multiple_of((slot * heads + first) * TILE, TILE), span)
            qt = qt_ref[:, at]
            gt = gt_ref[:, at]
            lows, grads = [], []
            for i in range(GROUP):
                h = first + i
                part = slice(i * TILE, (i + 1) * TILE)
                lse = lse_scr[h : h + 1, rows_of(slot, TILE)]
                delta = delta_scr[h : h + 1, rows_of(slot, TILE)]
                probs = jnp.exp2(nn(keys, qt[:, part]) * factor - lse)
                if masked:
                    probs = jnp.where(visible_mask(), probs, 0.0)
                slopes = nn(values, gt[:, part])
                grads.append((probs * (slopes - delta) * scale).astype(BF16))
                lows.append(probs.astype(BF16))
            low = jnp.concatenate(lows, axis=1)
            grad = jnp.concatenate(grads, axis=1)
            stash[n, :, first * TILE : first * TILE + span] = grad
            value_sum = value_sum + nt(gt, low)
            key_sum = key_sum + nt(qt, grad)
        dv_scr[:, rows_of(j, TILE)] = value_sum
        dk_scr[:, rows_of(j, TILE)] = key_sum

    for_tiles(blocks, work)

    z = own_z()
    dk_rows[...] = dk_scr[...].T
    dv_rows[...] = dv_scr[...].T

    def put(out, at, rel, pieces):
        for g in pieces:
            row = lax.rem(z + rel, ZS) * 8 + g * 8 * ZS
            for acc in (dk_rows, dv_rows):
                for blk in range(2):
                    start = pl.multiple_of(row + blk * (dk_rows.shape[0] // 2), 8)
                    out[at : at + 8, :] = acc[pl.ds(start, 8), :]
                    at += 8

    every = range(8)
    put(own, 0, 0, every)
    put(near_p, 0, 3, every)
    put(near_m, 0, 5, every)
    put(next_p, 0, 1, every)
    put(next_m, 0, 7, every)
    put(far_p, 0, 2, every)
    put(far_m, 0, 6, every)
    put(across, 0, 4, every)


def query_grad_kernel(
    blocks, kt_ref, stash, next_p, next_m, dq_near, dq_far, dq_core, out_p, out_m, dq_scr
):
    out_p[...] = next_p[...]
    out_m[...] = next_m[...]
    dq_scr[...] = jnp.zeros(dq_scr.shape, F32)
    span = stash.shape[2]

    def work(slot, j, masked, n):
        del masked
        kt = kt_ref[:, rows_of(j, TILE)]
        dq_scr[:, rows_of(slot, span)] += nn(kt, stash[n])

    for_tiles(blocks, work)
    ka = lax.axis_index("ka")
    half = TILE // 2
    heads = span // TILE
    places = ((dq_near, 0), (dq_core, 0), (dq_far, 0), (dq_core, kt_ref.shape[0]))
    for rel, (out, at) in enumerate(places):
        share = jnp.bitwise_xor(ka, rel)
        slot, side = share // 2, share % 2
        for h in range(heads):
            start = pl.multiple_of((slot * heads + h) * TILE + side * half, half)
            out[at : at + kt_ref.shape[0], h * half : (h + 1) * half] = dq_scr[:, pl.ds(start, half)]


def merge_kernel(far_p, got_np, far_m, got_nm, got_across, out_p, out_m):
    upward = lax.axis_index("ka") % 2 == 0
    out_p[...] = far_p[...] + got_np[...]
    out_m[...] = far_m[...] + got_nm[...]

    @pl.when(upward)
    def _():
        out_p[...] += got_across[...]

    @pl.when(jnp.logical_not(upward))
    def _():
        out_m[...] += got_across[...]


def sum_kernel(own, next_p, next_m, far_p, far_m, *outs):
    xh, y = own_head() // YS, own_head() % YS
    size = outs[0].shape[1]
    for rel, out in enumerate(outs):
        for i, x in enumerate((xh, 1 - xh)):
            rows = rows_of(x * YS + lax.rem(y + rel, YS), size)
            out[i] = (own[rows, :] + next_p[rows, :] + next_m[rows, :]) + (far_p[rows, :] + far_m[rows, :])


def cross_kernel(own, from1, from2, from3, out):
    for rel, part in enumerate((own, from1, from2, from3)):
        out[rel] = part[1]


def place_kernel(own, from1, from2, from3, crossed, after, dk_ref, dv_ref, scr):
    del after
    xh, y = own_head() // YS, own_head() % YS
    for rel, near in enumerate((own, from1, from2, from3)):
        from_y = lax.rem(y + YS - rel, YS)
        for part, from_x in ((near[0], xh), (crossed[rel], 1 - xh)):
            head = from_x * YS + from_y
            for kv in range(2):
                for blk in range(2):
                    at = (kv * 2 + blk) * 8
                    scr[kv, blk, :, pl.ds(head, 1), :] = part[at : at + 8, :].reshape(8, 1, part.shape[1])
    for kv, out in enumerate((dk_ref, dv_ref)):
        for blk in range(2):
            out[blk] = scr[kv, blk].reshape(64, out.shape[2]).astype(BF16)


def add_kernel(a_ref, b_ref, out_ref):
    out_ref[...] = a_ref[...] + b_ref[a_ref.shape[0] :]


def query_kernel(a_ref, b_ref, c_ref, out_ref, token_ref):
    token_ref[...] = jnp.zeros(token_ref.shape, F32)
    rows, width = out_ref.shape[0], a_ref.shape[0]
    for h in range(out_ref.shape[1] // width):
        part = slice(h * rows, (h + 1) * rows)
        total = a_ref[:, part] + b_ref[:width, part] + c_ref[:, part]
        out_ref[:, h * width : (h + 1) * width] = total.T.astype(BF16)


def array(shape, dtype=F32):
    return jax.ShapeDtypeStruct(shape, dtype)


SMALL = pl.BlockSpec(memory_space=pltpu.VMEM)
SCALARS = pl.BlockSpec(memory_space=pltpu.SMEM)
LARGE = pl.BlockSpec(memory_space=pltpu.HBM)


def cost(us):
    return pl.CostEstimate(flops=int(us * 1.15e9), bytes_accessed=0, transcendentals=0)


def vmem(mib):
    return pltpu.CompilerParams(vmem_limit_bytes=int(mib * 2**20))


def row_stats(blocks, queries, grad_out, keys, values):
    _, key_count, width = keys.shape
    query_count = queries.shape[0]
    heads = queries.shape[1] // width
    return pl.pallas_call(
        functools.partial(stat_kernel, width),
        out_shape=array((2 * heads, query_count)),
        in_specs=[SCALARS] + [LARGE] * 4,
        out_specs=SMALL,
        scratch_shapes=[pltpu.VMEM(queries.shape, BF16)] * 2
        + [pltpu.VMEM((key_count, width), BF16)] * 2
        + [pltpu.VMEM((heads, 2, 8, TILE), F32)] * 3
        + [pltpu.SemaphoreType.DMA((6,))],
        compiler_params=vmem(24),
        name="row_stats",
    )(blocks, queries, grad_out, keys, values)


def turned_inputs(queries, grad_out, keys, values):
    _, key_count, width = keys.shape
    turned = array((width, queries.size // width), BF16)
    own = array((key_count, width), BF16)
    return pl.pallas_call(
        turn_kernel,
        out_shape=[turned, turned, own, own, array((width, key_count), BF16)],
        in_specs=[LARGE] * 4,
        out_specs=[SMALL] * 5,
        scratch_shapes=[pltpu.VMEM(queries.shape, BF16)] * 2 + [pltpu.SemaphoreType.DMA((6,))],
        compiler_params=vmem(16),
        cost_estimate=cost(3),
        name="turn_inputs",
    )(queries, grad_out, keys, values)


def key_gradients(blocks, turned_q, turned_g, keys, values, stats):
    key_count, width = keys.shape
    heads = stats[0].shape[0] // 2
    query_count = stats[0].shape[1]
    chunk = (256, width)
    shapes = [chunk] * 8
    return pl.pallas_call(
        functools.partial(grad_kernel, width),
        out_shape=[array((5, TILE, heads * TILE), BF16)] + [array(s) for s in shapes],
        in_specs=[SCALARS] + [SMALL] * 8,
        out_specs=[SMALL] * 9,
        scratch_shapes=[pltpu.VMEM((heads, query_count), F32)] * 2
        + [pltpu.VMEM((width, key_count), F32)] * 2
        + [pltpu.VMEM((key_count, width), F32)] * 2,
        compiler_params=vmem(24),
        name="key_grads",
    )(blocks, turned_q, turned_g, keys, values, *stats)


def query_gradients(blocks, turned_k, stash, next_p, next_m):
    width = turned_k.shape[0]
    span = stash.shape[2]
    return pl.pallas_call(
        query_grad_kernel,
        out_shape=[array((width, span // 2))] * 2 + [array((2 * width, span // 2))] + [array(next_p.shape)] * 2,
        in_specs=[SCALARS] + [SMALL] * 4,
        out_specs=[SMALL] * 5,
        scratch_shapes=[pltpu.VMEM((width, 2 * span), F32)],
        compiler_params=vmem(16),
        cost_estimate=cost(2.5),
        name="query_grads",
    )(blocks, turned_k, stash, next_p, next_m)


def on_device(queries, keys, values, grad_out, query_blocks):
    queries, grad_out, keys, values, blocks = (
        pltpu.with_memory_space_constraint(x, pltpu.HBM) for x in (queries, grad_out, keys, values, query_blocks)
    )
    width = keys.shape[2]
    query_count = queries.shape[0]
    pb_size = lax.axis_size("pb")

    def across_ka(x, by):
        return lax.ppermute(x, "ka", [(a, a ^ by) for a in range(4)])

    own_stats = row_stats(blocks, queries, grad_out, keys, values)
    stats = [own_stats] + [across_ka(own_stats, by) for by in (2, 3, 1)]
    turned_q, turned_g, own_k, own_v, turned_k = turned_inputs(queries, grad_out, keys, values)
    stash, own, near_p, near_m, next_p, next_m, far_p, far_m, across = key_gradients(
        blocks, turned_q, turned_g, own_k, own_v, stats
    )

    def along_y(x, by):
        return lax.ppermute(
            x, "pb", [(p, (p // (ZS * YS) * YS + (p // ZS + by) % YS) * ZS + p % ZS) for p in range(pb_size)]
        )

    def along_z(x, by):
        return lax.ppermute(x, "pb", [(p, p // ZS * ZS + (p + by) % ZS) for p in range(pb_size)])

    pairs = []
    for p in range(pb_size):
        for a in range(4):
            there = p // ZS * ZS + (p + (2 if a % 2 == 0 else ZS - 2)) % ZS
            pairs.append((p * 4 + a, there * 4 + a))
    got_across = lax.ppermute(across, ("pb", "ka"), pairs)
    got_np = along_z(near_p, 1)
    got_nm = along_z(near_m, ZS - 1)

    dq_near, dq_far, dq_core, next_p, next_m = query_gradients(blocks, turned_k, stash, next_p, next_m)
    next_p = along_z(next_p, 1)
    next_m = along_z(next_m, ZS - 1)
    got_core = across_ka(dq_core, 1)
    for_other = pl.pallas_call(
        add_kernel,
        out_shape=array(dq_far.shape),
        in_specs=[SMALL] * 2,
        out_specs=SMALL,
        compiler_params=vmem(4),
        name="add_queries",
    )(dq_far, got_core)
    got_far = across_ka(for_other, 2)
    far_p, far_m = pl.pallas_call(
        merge_kernel,
        out_shape=[array(far_p.shape), array(far_m.shape)],
        in_specs=[SMALL] * 5,
        out_specs=[SMALL] * 2,
        compiler_params=vmem(8),
        cost_estimate=cost(10),
        name="merge",
    )(far_p, got_np, far_m, got_nm, got_across)
    got_fp = along_z(far_p, 2)
    got_fm = along_z(far_m, ZS - 2)
    parts = pl.pallas_call(
        sum_kernel,
        out_shape=[array((2, 32, width))] * YS,
        in_specs=[SMALL] * 5,
        out_specs=[SMALL] * YS,
        compiler_params=vmem(8),
        name="add_parts",
    )(own, next_p, next_m, got_fp, got_fm)
    parts = [parts[0]] + [along_y(parts[k], k) for k in range(1, YS)]
    crossed = pl.pallas_call(
        cross_kernel,
        out_shape=array((YS, 32, width)),
        in_specs=[SMALL] * YS,
        out_specs=SMALL,
        compiler_params=vmem(4),
        cost_estimate=cost(3),
        name="cross_parts",
    )(*parts)
    crossed = lax.ppermute(crossed, "pb", [(p, (p + pb_size // 2) % pb_size) for p in range(pb_size)])
    grad_queries, token = pl.pallas_call(
        query_kernel,
        out_shape=[array((query_count // 4, queries.shape[1]), BF16), array((8, 128))],
        in_specs=[SMALL] * 3,
        out_specs=[SMALL] * 2,
        compiler_params=vmem(8),
        name="finish_queries",
    )(dq_near, got_core, got_far)
    grad_keys, grad_values = pl.pallas_call(
        place_kernel,
        out_shape=[array((2, 64, width), BF16)] * 2,
        in_specs=[SMALL] * (YS + 1) + [pl.BlockSpec(memory_space=pl.ANY)],
        out_specs=[SMALL] * 2,
        scratch_shapes=[pltpu.VMEM((2, 2, 8, 8, width), F32)],
        compiler_params=vmem(4),
        cost_estimate=cost(3),
        name="place_rows",
    )(*parts, crossed, token)

    return grad_queries, grad_keys, grad_values


def solution(mesh):
    placed = (P("pb", None), P(None, "ka", None), P(None, "ka", None), P("pb", None), P("pb"))
    return jax.shard_map(
        on_device,
        mesh=mesh,
        in_specs=placed,
        out_specs=(P(("pb", "ka"), None), P("ka", "pb", None), P("ka", "pb", None)),
        check_vma=False,
    )
```

```python
import functools
import math

import jax
import jax.numpy as jnp
from jax import lax
from jax.experimental import pallas as pl
from jax.experimental.pallas import tpu as pltpu
from jax.sharding import PartitionSpec as P

NEG = -1e30
HIDDEN = -2e30
TILE = 256
GROUP = 4
ZS = 8
YS = 4
F32 = jnp.float32
BF16 = jnp.bfloat16


def nt(a, b):
    return lax.dot_general(a, b, (((1,), (1,)), ((), ())), preferred_element_type=F32)


def nn(a, b):
    return jnp.dot(a, b, preferred_element_type=F32)


def own_head():
    return lax.axis_index("pb") // ZS


def own_z():
    return lax.axis_index("pb") % ZS


def for_tiles(blocks, work, before_slot=None):
    ka = lax.axis_index("ka")

    def step(u, n):
        slot = u // 4
        j = u % 4
        place = jnp.where(j < 2, 2 * ka + j, 2 * (7 - ka) + j - 2)
        block = blocks[slot]
        if before_slot is not None:
            pl.when(u == 4)(functools.partial(before_slot, 1))

        @pl.when(place < block)
        def _():
            work(slot, j, False, n)

        @pl.when(place == block)
        def _():
            work(slot, j, True, n)

        return n + jnp.where(place <= block, 1, 0)

    if before_slot is not None:
        before_slot(0)
    lax.fori_loop(0, 8, step, 0)


def rows_of(index, size):
    return pl.ds(pl.multiple_of(index * size, size), size)


def visible_mask():
    shape = (TILE, TILE)
    return lax.broadcasted_iota(jnp.int32, shape, 0) <= lax.broadcasted_iota(jnp.int32, shape, 1)


def slot_rows(slot):
    return slice(slot * TILE, (slot + 1) * TILE)


def copies_in(q_hbm, g_hbm, k_hbm, v_hbm, q_ref, g_ref, k_ref, v_ref, sems):
    head = own_head()
    pairs = [(k_hbm.at[head], k_ref), (v_hbm.at[head], v_ref)]
    for slot in range(2):
        rows = slot_rows(slot)
        pairs += [(q_hbm.at[rows], q_ref.at[rows]), (g_hbm.at[rows], g_ref.at[rows])]
    return [pltpu.make_async_copy(src, dst, sems.at[i]) for i, (src, dst) in enumerate(pairs)]


def stat_kernel(
    width, blocks, q_hbm, g_hbm, k_hbm, v_hbm, out_ref,
    q_ref, g_ref, k_ref, v_ref, m_scr, l_scr, d_scr, sems,
):
    copies = copies_in(q_hbm, g_hbm, k_hbm, v_hbm, q_ref, g_ref, k_ref, v_ref, sems)
    for copy in copies:
        copy.start()
    factor = width**-0.5 * math.log2(math.e)
    heads = out_ref.shape[0] // 2
    m_scr[...] = jnp.full(m_scr.shape, NEG, F32)
    l_scr[...] = jnp.zeros(l_scr.shape, F32)
    d_scr[...] = jnp.zeros(d_scr.shape, F32)

    def before_slot(slot):
        for copy in copies[:2] * (slot == 0) + copies[2 + 2 * slot : 4 + 2 * slot]:
            copy.wait()

    def work(slot, j, masked, n):
        keys = k_ref[rows_of(j, TILE), :]
        values = v_ref[rows_of(j, TILE), :]
        for h in range(heads):
            cols = slice(h * width, (h + 1) * width)
            scores = nt(keys, q_ref[rows_of(slot, TILE), cols]) * factor
            if masked:
                scores = jnp.where(visible_mask(), scores, HIDDEN)
            scores = scores.reshape(TILE // 8, 8, TILE)
            slopes = nt(values, g_ref[rows_of(slot, TILE), cols]).reshape(TILE // 8, 8, TILE)
            old = m_scr[h, slot]
            new = jnp.maximum(old, jnp.max(scores, axis=0))
            weights = jnp.exp2(scores - new[None])
            shrink = jnp.exp2(old - new)
            m_scr[h, slot] = new
            l_scr[h, slot] = l_scr[h, slot] * shrink + jnp.sum(weights, axis=0)
            d_scr[h, slot] = d_scr[h, slot] * shrink + jnp.sum(weights * slopes, axis=0)

    for_tiles(blocks, work, before_slot)
    for h in range(heads):
        for slot in range(2):
            cols = slot_rows(slot)
            m = m_scr[h, slot]
            top = jnp.max(m, axis=0, keepdims=True)
            shrink = jnp.exp2(m - top)
            total = jnp.sum(l_scr[h, slot] * shrink, axis=0, keepdims=True)
            dotted = jnp.sum(d_scr[h, slot] * shrink, axis=0, keepdims=True)
            out_ref[h : h + 1, cols] = top + jnp.log2(total)
            out_ref[heads + h : heads + h + 1, cols] = jnp.where(total > 0, dotted / total, 0.0)


def turn_kernel(q_ref, g_ref, k_ref, qt_ref, gt_ref, kt_ref):
    width = k_ref.shape[1]
    heads = q_ref.shape[1] // width
    kt_ref[...] = k_ref[...].T
    for slot in range(2):
        for h in range(heads):
            cols = slice(h * width, (h + 1) * width)
            at = (slot * heads + h) * TILE
            qt_ref[:, at : at + TILE] = q_ref[slot_rows(slot), cols].T
            gt_ref[:, at : at + TILE] = g_ref[slot_rows(slot), cols].T


def grad_kernel(
    width, blocks, qt_ref, gt_ref, k_ref, v_ref, *refs,
):
    grad_body(width, blocks, qt_ref, gt_ref, k_ref, v_ref, refs[:4], *refs[4:])


def grad_body(
    width, blocks, qt_ref, gt_ref, k_ref, v_ref, stats,
    stash, own, near_p, near_m, next_p, next_m, far_p, far_m, across,
    lse_scr, delta_scr, dk_scr, dv_scr, dk_rows, dv_rows,
):
    scale = width**-0.5
    factor = scale * math.log2(math.e)
    heads = lse_scr.shape[0]
    top = stats[0][:heads]
    for stat in stats[1:]:
        top = jnp.maximum(top, stat[:heads])
    total = jnp.zeros(top.shape, F32)
    dotted = jnp.zeros(top.shape, F32)
    for stat in stats:
        share = jnp.exp2(stat[:heads] - top)
        total += share
        dotted += stat[heads:] * share
    lse_scr[...] = top + jnp.log2(total)
    delta_scr[...] = dotted / total
    dk_scr[...] = jnp.zeros(dk_scr.shape, F32)
    dv_scr[...] = jnp.zeros(dv_scr.shape, F32)

    def work(slot, j, masked, n):
        keys = k_ref[rows_of(j, TILE), :]
        values = v_ref[rows_of(j, TILE), :]
        span = GROUP * TILE
        value_sum = dv_scr[:, rows_of(j, TILE)]
        key_sum = dk_scr[:, rows_of(j, TILE)]
        for first in range(0, heads, GROUP):
            at = pl.ds(pl.multiple_of((slot * heads + first) * TILE, TILE), span)
            qt = qt_ref[:, at]
            gt = gt_ref[:, at]
            lows, grads = [], []
            for i in range(GROUP):
                h = first + i
                part = slice(i * TILE, (i + 1) * TILE)
                lse = lse_scr[h : h + 1, rows_of(slot, TILE)]
                delta = delta_scr[h : h + 1, rows_of(slot, TILE)]
                probs = jnp.exp2(nn(keys, qt[:, part]) * factor - lse)
                if masked:
                    probs = jnp.where(visible_mask(), probs, 0.0)
                slopes = nn(values, gt[:, part])
                grads.append((probs * (slopes - delta) * scale).astype(BF16))
                lows.append(probs.astype(BF16))
            low = jnp.concatenate(lows, axis=1)
            grad = jnp.concatenate(grads, axis=1)
            stash[n, :, first * TILE : first * TILE + span] = grad
            value_sum = value_sum + nt(gt, low)
            key_sum = key_sum + nt(qt, grad)
        dv_scr[:, rows_of(j, TILE)] = value_sum
        dk_scr[:, rows_of(j, TILE)] = key_sum

    for_tiles(blocks, work)

    z = own_z()
    dk_rows[...] = dk_scr[...].T
    dv_rows[...] = dv_scr[...].T

    def put(out, at, rel, pieces):
        for g in pieces:
            row = lax.rem(z + rel, ZS) * 8 + g * 8 * ZS
            for acc in (dk_rows, dv_rows):
                for blk in range(2):
                    start = pl.multiple_of(row + blk * (dk_rows.shape[0] // 2), 8)
                    out[at : at + 8, :] = acc[pl.ds(start, 8), :]
                    at += 8

    every = range(8)
    put(own, 0, 0, every)
    put(near_p, 0, 3, every)
    put(near_m, 0, 5, every)
    put(next_p, 0, 1, every)
    put(next_m, 0, 7, every)
    put(far_p, 0, 2, every)
    put(far_m, 0, 6, every)
    put(across, 0, 4, every)


def query_grad_kernel(
    blocks, kt_ref, stash, next_p, next_m, dq_near, dq_far, dq_core, out_p, out_m, dq_scr
):
    out_p[...] = next_p[...]
    out_m[...] = next_m[...]
    dq_scr[...] = jnp.zeros(dq_scr.shape, F32)
    span = stash.shape[2]

    def work(slot, j, masked, n):
        del masked
        kt = kt_ref[:, rows_of(j, TILE)]
        dq_scr[:, rows_of(slot, span)] += nn(kt, stash[n])

    for_tiles(blocks, work)
    ka = lax.axis_index("ka")
    half = TILE // 2
    heads = span // TILE
    places = ((dq_near, 0), (dq_core, 0), (dq_far, 0), (dq_core, kt_ref.shape[0]))
    for rel, (out, at) in enumerate(places):
        share = jnp.bitwise_xor(ka, rel)
        slot, side = share // 2, share % 2
        for h in range(heads):
            start = pl.multiple_of((slot * heads + h) * TILE + side * half, half)
            out[at : at + kt_ref.shape[0], h * half : (h + 1) * half] = dq_scr[:, pl.ds(start, half)]


def merge_kernel(far_p, got_np, far_m, got_nm, got_across, out_p, out_m):
    upward = lax.axis_index("ka") % 2 == 0
    out_p[...] = far_p[...] + got_np[...]
    out_m[...] = far_m[...] + got_nm[...]

    @pl.when(upward)
    def _():
        out_p[...] += got_across[...]

    @pl.when(jnp.logical_not(upward))
    def _():
        out_m[...] += got_across[...]


def sum_kernel(own, next_p, next_m, far_p, far_m, *outs):
    xh, y = own_head() // YS, own_head() % YS
    size = outs[0].shape[1]
    for rel, out in enumerate(outs):
        for i, x in enumerate((xh, 1 - xh)):
            rows = rows_of(x * YS + lax.rem(y + rel, YS), size)
            out[i] = (own[rows, :] + next_p[rows, :] + next_m[rows, :]) + (far_p[rows, :] + far_m[rows, :])


def cross_kernel(own, from1, from2, from3, out):
    for rel, part in enumerate((own, from1, from2, from3)):
        out[rel] = part[1]


def place_kernel(own, from1, from2, from3, crossed, after, dk_ref, dv_ref, scr):
    del after
    xh, y = own_head() // YS, own_head() % YS
    for rel, near in enumerate((own, from1, from2, from3)):
        from_y = lax.rem(y + YS - rel, YS)
        for part, from_x in ((near[0], xh), (crossed[rel], 1 - xh)):
            head = from_x * YS + from_y
            for kv in range(2):
                for blk in range(2):
                    at = (kv * 2 + blk) * 8
                    scr[kv, blk, :, pl.ds(head, 1), :] = part[at : at + 8, :].reshape(8, 1, part.shape[1])
    for kv, out in enumerate((dk_ref, dv_ref)):
        for blk in range(2):
            out[blk] = scr[kv, blk].reshape(64, out.shape[2]).astype(BF16)


def add_kernel(a_ref, b_ref, out_ref):
    out_ref[...] = a_ref[...] + b_ref[a_ref.shape[0] :]


def query_kernel(a_ref, b_ref, c_ref, out_ref, token_ref):
    token_ref[...] = jnp.zeros(token_ref.shape, F32)
    rows, width = out_ref.shape[0], a_ref.shape[0]
    for h in range(out_ref.shape[1] // width):
        part = slice(h * rows, (h + 1) * rows)
        total = a_ref[:, part] + b_ref[:width, part] + c_ref[:, part]
        out_ref[:, h * width : (h + 1) * width] = total.T.astype(BF16)


def array(shape, dtype=F32):
    return jax.ShapeDtypeStruct(shape, dtype)


SMALL = pl.BlockSpec(memory_space=pltpu.VMEM)
SCALARS = pl.BlockSpec(memory_space=pltpu.SMEM)
LARGE = pl.BlockSpec(memory_space=pltpu.HBM)


def cost(us):
    return pl.CostEstimate(flops=int(us * 1.15e9), bytes_accessed=0, transcendentals=0)


def vmem(mib):
    return pltpu.CompilerParams(vmem_limit_bytes=int(mib * 2**20))


def row_stats(blocks, queries, grad_out, keys, values):
    _, key_count, width = keys.shape
    query_count = queries.shape[0]
    heads = queries.shape[1] // width
    own = array((key_count, width), BF16)
    rows = array(queries.shape, BF16)
    return pl.pallas_call(
        functools.partial(stat_kernel, width),
        out_shape=[array((2 * heads, query_count)), rows, rows, own, own],
        in_specs=[SCALARS] + [LARGE] * 4,
        out_specs=[SMALL] * 5,
        scratch_shapes=[pltpu.VMEM((heads, 2, 8, TILE), F32)] * 3 + [pltpu.SemaphoreType.DMA((6,))],
        compiler_params=vmem(24),
        name="row_stats",
    )(blocks, queries, grad_out, keys, values)


def turned_inputs(queries, grad_out, keys):
    key_count, width = keys.shape
    turned = array((width, queries.size // width), BF16)
    return pl.pallas_call(
        turn_kernel,
        out_shape=[turned, turned, array((width, key_count), BF16)],
        in_specs=[SMALL] * 3,
        out_specs=[SMALL] * 3,
        compiler_params=vmem(16),
        cost_estimate=cost(3),
        name="turn_inputs",
    )(queries, grad_out, keys)


def key_gradients(blocks, turned_q, turned_g, keys, values, stats):
    key_count, width = keys.shape
    heads = stats[0].shape[0] // 2
    query_count = stats[0].shape[1]
    chunk = (256, width)
    shapes = [chunk] * 8
    return pl.pallas_call(
        functools.partial(grad_kernel, width),
        out_shape=[array((5, TILE, heads * TILE), BF16)] + [array(s) for s in shapes],
        in_specs=[SCALARS] + [SMALL] * 8,
        out_specs=[SMALL] * 9,
        scratch_shapes=[pltpu.VMEM((heads, query_count), F32)] * 2
        + [pltpu.VMEM((width, key_count), F32)] * 2
        + [pltpu.VMEM((key_count, width), F32)] * 2,
        compiler_params=vmem(24),
        name="key_grads",
    )(blocks, turned_q, turned_g, keys, values, *stats)


def query_gradients(blocks, turned_k, stash, next_p, next_m):
    width = turned_k.shape[0]
    span = stash.shape[2]
    return pl.pallas_call(
        query_grad_kernel,
        out_shape=[array((width, span // 2))] * 2 + [array((2 * width, span // 2))] + [array(next_p.shape)] * 2,
        in_specs=[SCALARS] + [SMALL] * 4,
        out_specs=[SMALL] * 5,
        scratch_shapes=[pltpu.VMEM((width, 2 * span), F32)],
        compiler_params=vmem(16),
        cost_estimate=cost(2.5),
        name="query_grads",
    )(blocks, turned_k, stash, next_p, next_m)


def on_device(queries, keys, values, grad_out, query_blocks):
    queries, grad_out, keys, values, blocks = (
        pltpu.with_memory_space_constraint(x, pltpu.HBM) for x in (queries, grad_out, keys, values, query_blocks)
    )
    width = keys.shape[2]
    query_count = queries.shape[0]
    pb_size = lax.axis_size("pb")

    def across_ka(x, by):
        return lax.ppermute(x, "ka", [(a, a ^ by) for a in range(4)])

    own_stats, own_q, own_g, own_k, own_v = row_stats(blocks, queries, grad_out, keys, values)
    stats = [own_stats] + [across_ka(own_stats, by) for by in (2, 3, 1)]
    turned_q, turned_g, turned_k = turned_inputs(own_q, own_g, own_k)
    stash, own, near_p, near_m, next_p, next_m, far_p, far_m, across = key_gradients(
        blocks, turned_q, turned_g, own_k, own_v, stats
    )

    def along_y(x, by):
        return lax.ppermute(
            x, "pb", [(p, (p // (ZS * YS) * YS + (p // ZS + by) % YS) * ZS + p % ZS) for p in range(pb_size)]
        )

    def along_z(x, by):
        return lax.ppermute(x, "pb", [(p, p // ZS * ZS + (p + by) % ZS) for p in range(pb_size)])

    pairs = []
    for p in range(pb_size):
        for a in range(4):
            there = p // ZS * ZS + (p + (2 if a % 2 == 0 else ZS - 2)) % ZS
            pairs.append((p * 4 + a, there * 4 + a))
    got_across = lax.ppermute(across, ("pb", "ka"), pairs)
    got_np = along_z(near_p, 1)
    got_nm = along_z(near_m, ZS - 1)

    dq_near, dq_far, dq_core, next_p, next_m = query_gradients(blocks, turned_k, stash, next_p, next_m)
    next_p = along_z(next_p, 1)
    next_m = along_z(next_m, ZS - 1)
    got_core = across_ka(dq_core, 1)
    for_other = pl.pallas_call(
        add_kernel,
        out_shape=array(dq_far.shape),
        in_specs=[SMALL] * 2,
        out_specs=SMALL,
        compiler_params=vmem(4),
        name="add_queries",
    )(dq_far, got_core)
    got_far = across_ka(for_other, 2)
    far_p, far_m = pl.pallas_call(
        merge_kernel,
        out_shape=[array(far_p.shape), array(far_m.shape)],
        in_specs=[SMALL] * 5,
        out_specs=[SMALL] * 2,
        compiler_params=vmem(8),
        cost_estimate=cost(10),
        name="merge",
    )(far_p, got_np, far_m, got_nm, got_across)
    got_fp = along_z(far_p, 2)
    got_fm = along_z(far_m, ZS - 2)
    parts = pl.pallas_call(
        sum_kernel,
        out_shape=[array((2, 32, width))] * YS,
        in_specs=[SMALL] * 5,
        out_specs=[SMALL] * YS,
        compiler_params=vmem(8),
        name="add_parts",
    )(own, next_p, next_m, got_fp, got_fm)
    parts = [parts[0]] + [along_y(parts[k], k) for k in range(1, YS)]
    crossed = pl.pallas_call(
        cross_kernel,
        out_shape=array((YS, 32, width)),
        in_specs=[SMALL] * YS,
        out_specs=SMALL,
        compiler_params=vmem(4),
        cost_estimate=cost(3),
        name="cross_parts",
    )(*parts)
    crossed = lax.ppermute(crossed, "pb", [(p, (p + pb_size // 2) % pb_size) for p in range(pb_size)])
    grad_queries, token = pl.pallas_call(
        query_kernel,
        out_shape=[array((query_count // 4, queries.shape[1]), BF16), array((8, 128))],
        in_specs=[SMALL] * 3,
        out_specs=[SMALL] * 2,
        compiler_params=vmem(8),
        name="finish_queries",
    )(dq_near, got_core, got_far)
    grad_keys, grad_values = pl.pallas_call(
        place_kernel,
        out_shape=[array((2, 64, width), BF16)] * 2,
        in_specs=[SMALL] * (YS + 1) + [pl.BlockSpec(memory_space=pl.ANY)],
        out_specs=[SMALL] * 2,
        scratch_shapes=[pltpu.VMEM((2, 2, 8, 8, width), F32)],
        compiler_params=vmem(4),
        cost_estimate=cost(3),
        name="place_rows",
    )(*parts, crossed, token)

    return grad_queries, grad_keys, grad_values


def solution(mesh):
    placed = (P("pb", None), P(None, "ka", None), P(None, "ka", None), P("pb", None), P("pb"))
    return jax.shard_map(
        on_device,
        mesh=mesh,
        in_specs=placed,
        out_specs=(P(("pb", "ka"), None), P("ka", "pb", None), P("ka", "pb", None)),
        check_vma=False,
    )
```
